256 devices in a mesh: gx: 16 (over x, z_lo, core), gy: 16 (over z_hi, y).
Axes of the slice: x: 4, y: 4, z: 8 (z_hi: 4, z_lo: 2; z = z_hi * 2 + z_lo), core: 2. Of those that a mesh axis runs over, the one named last changes fastest.
Arguments:
- p_now: float32 [256, 256, 128], P('gx', 'gy'), may hold values from -6 to 6
- p_prev: float32 [256, 256, 128], P('gx', 'gy'), may hold values from -6 to 6
- water_coef: float32 [256, 256, 128], P('gx', 'gy'), may hold values from 0.05 to 0.3
- seafloor: int32 [256, 512], P('gx', 'gy'), may hold values from -1 to 127, as said below
- u_now: float32 [3, 256, 512, 128], P(None, 'gx', 'gy'), may hold values from -6 to 6
- u_prev: float32 [3, 256, 512, 128], P(None, 'gx', 'gy'), may hold values from -6 to 6
- shear: float32 [256, 512, 128], P('gx', 'gy'), may hold values from 0.03 to 0.1
- bulk: float32 [256, 512, 128], P('gx', 'gy'), may hold values from 0.03 to 0.1
- recv_field: bfloat16 [4, 256, 512, 128], P(None, 'gx', 'gy'), may hold values from -6 to 6
Outputs:
- pressure_out: float32 [256, 256, 128], P('gx', 'gy')
- displacement_out: float32 [3, 256, 512, 128], P(None, 'gx', 'gy')
- image: bfloat16 [21, 256, 512, 128], P(None, 'gx', 'gy')
The draws below stay inside these ranges and needn't reach their ends.
Inputs may be any that keep to these rules, and one draw needn't show every extreme that they name: For every column exactly one of its two rows (depth halves) is 0 or more (the seafloor cell within that half); the other is -1.
All inputs are finite; a program needn't handle non-finite values.
Results may differ from the reference program's by a relative error of at most 0.001.
Values sent between devices are 32-bit elements; how exact they have to be, the bound alone decides.
No kernel may reach another device: no remote copies, remote signals or barrier semaphores. Data moves between devices by JAX's collectives and lax.ppermute only.
A program may use at most 128 MiB of HBM per device.

```python
import math
import jax
import jax.numpy as jnp
from jax import lax

BY = 16
WZ = 128
SH = 128
LAG = 10
STEPS = 4
NX = 256
NY = 256


def draw_seafloor(key, part):
    key = jax.random.fold_in(key, 7)
    seafloor_depth = jax.random.randint(key, (NX, NY), SH // 2, SH + SH // 2)
    seafloor_depth = seafloor_depth.at[0, 0].set(SH - 1)
    upper_half = jnp.where(seafloor_depth < SH, seafloor_depth, -1)
    lower_half = jnp.where(seafloor_depth >= SH, seafloor_depth - SH, -1)
    blocks = NY // (2 * BY)
    upper_grouped = upper_half.reshape(NX, blocks, 2 * BY)
    lower_grouped = lower_half.reshape(NX, blocks, 2 * BY)
    stacked = jnp.stack([upper_grouped, lower_grouped], axis=2)
    return stacked.reshape(NX, 2 * NY).astype(jnp.int32)


def level_of(rng, shape, cuts, low, top_value):
    def one(axis_at, blocks):
        steps = jax.random.uniform(jax.random.fold_in(jax.random.fold_in(rng, 6), axis_at), (blocks,), jnp.float32, low / len(cuts), top_value / len(cuts))
        return jnp.repeat(jnp.exp(steps), shape[axis_at] // blocks).reshape((-1,) + (1,) * (len(shape) - axis_at - 1))

    factor_of = one(*cuts[0])
    for cut in cuts[1:]:
        factor_of = factor_of * one(*cut)
    return factor_of


def scatter_about(rng, shape, width, most, cuts=(), kind=jnp.bfloat16):
    values = width * jax.random.normal(rng, shape, jnp.float32)
    if cuts:
        values = values * level_of(rng, shape, cuts, -0.22, 0.18)
    return jnp.clip(values, -most, most).astype(kind)


def setup_inputs(seed: int = 0) -> dict:
    seeds = jax.random.split(jax.random.key(seed), 10)
    return {
        "p_now": scatter_about(seeds[0], (NX, NY, WZ), 1.0, 6.0, ((0, 16), (1, 16)), jnp.float32),
        "p_prev": scatter_about(seeds[1], (NX, NY, WZ), 1.0, 6.0, ((0, 16), (1, 16)), jnp.float32),
        "water_coef": jnp.clip(jnp.exp(math.log(0.3) - 1.7917595 * jax.random.uniform(seeds[2], (NX, NY, WZ), jnp.float32) ** level_of(seeds[2], (NX, NY, WZ), ((0, 16), (1, 16)), -0.2, 0.2)), 0.05, 0.3),
        "seafloor": draw_seafloor(jax.random.fold_in(seeds[9], 71), 0),
        "u_now": scatter_about(seeds[4], (3, NX, 2 * NY, SH), 1.0, 6.0, ((1, 16), (2, 16)), jnp.float32),
        "u_prev": scatter_about(seeds[5], (3, NX, 2 * NY, SH), 1.0, 6.0, ((1, 16), (2, 16)), jnp.float32),
        "shear": jnp.clip(jnp.exp(math.log(0.1) - 1.2039728 * jax.random.uniform(seeds[6], (NX, 2 * NY, SH), jnp.float32) ** level_of(seeds[6], (NX, 2 * NY, SH), ((0, 16), (1, 16)), -0.2, 0.2)), 0.03, 0.1),
        "bulk": jnp.clip(jnp.exp(math.log(0.1) - 1.2039728 * jax.random.uniform(seeds[7], (NX, 2 * NY, SH), jnp.float32) ** level_of(seeds[7], (NX, 2 * NY, SH), ((0, 16), (1, 16)), -0.2, 0.2)), 0.03, 0.1),
        "recv_field": scatter_about(seeds[8], (STEPS, NX, 2 * NY, SH), 1.0, 6.0, ((1, 16), (2, 16))),
    }


load_factor = 0.5


def shifted(padded, step_x, step_y, step_z):
    size_x = padded.shape[-3] - 2
    size_y = padded.shape[-2] - 2
    size_z = padded.shape[-1] - 2
    return padded[..., 1 + step_x:1 + step_x + size_x, 1 + step_y:1 + step_y + size_y, 1 + step_z:1 + step_z + size_z]


def moved(padded, first_step, second_step):
    return shifted(padded, first_step[0] + second_step[0], first_step[1] + second_step[1], first_step[2] + second_step[2])


def negated(offset):
    return (-offset[0], -offset[1], -offset[2])


def elastic(padded, shear_field, bulk_field):
    anchor = (0, 0, 0)
    unit_steps = ((1, 0, 0), (0, 1, 0), (0, 0, 1))
    centre = moved(padded, anchor, anchor)
    laplace = -6.0 * centre
    for unit_step in unit_steps:
        laplace = laplace + moved(padded, unit_step, anchor) + moved(padded, negated(unit_step), anchor)
    pieces = []
    for first_axis in range(3):
        running = jnp.zeros_like(centre[0])
        for second_axis in range(3):
            component = padded[second_axis]
            step_a = unit_steps[first_axis]
            step_b = unit_steps[second_axis]
            if first_axis == second_axis:
                summand = moved(component, step_a, anchor) + moved(component, negated(step_a), anchor) - 2.0 * moved(component, anchor, anchor)
            else:
                summand = 0.25 * (moved(component, step_a, step_b) - moved(component, step_a, negated(step_b)) - moved(component, negated(step_a), step_b) + moved(component, negated(step_a), negated(step_b)))
            running = running + summand
        pieces.append(running)
    return shear_field * laplace + bulk_field * jnp.stack(pieces)


def to_depth(field):
    leading = field.shape[:-2]
    blocks = NY // (2 * BY)
    grouped = field.reshape(leading + (blocks, 2, 2 * BY, SH))
    upper = grouped[..., 0, :, :].reshape(leading + (NY, SH))
    lower = grouped[..., 1, :, :].reshape(leading + (NY, SH))
    return jnp.concatenate([upper, lower], axis=-1)


def from_depth(field):
    leading = field.shape[:-2]
    blocks = NY // (2 * BY)
    grouped = field.reshape(leading + (blocks, 2 * BY, 2 * SH))
    stacked = jnp.stack([grouped[..., :SH], grouped[..., SH:]], axis=-3)
    return stacked.reshape(leading + (2 * NY, SH))


def reference(p_now, p_prev, water_coef, seafloor, u_now, u_prev, shear, bulk, recv_field):
    blocks = NY // (2 * BY)
    grouped_floor = seafloor.reshape(NX, blocks, 2, 2 * BY)
    upper_rows = grouped_floor[:, :, 0, :].reshape(NX, NY)
    lower_rows = grouped_floor[:, :, 1, :].reshape(NX, NY)
    level = jnp.where(upper_rows >= 0, upper_rows, lower_rows + SH).astype(jnp.int32)
    depth_cells = jnp.arange(2 * SH, dtype=jnp.int32)
    solid_mask = (depth_cells[None, None, :] >= level[:, :, None]).astype(jnp.float32)
    contact = (depth_cells[None, None, :] == level[:, :, None]).astype(jnp.float32)
    current = to_depth(u_now) * solid_mask
    previous = to_depth(u_prev) * solid_mask
    shear_depth = to_depth(shear)
    bulk_depth = to_depth(bulk)
    pressure = p_now
    pressure_old = p_prev
    lifted = []
    for step_index in range(STEPS):
        velocity = jnp.sum((current[2] - previous[2]) * contact, axis=-1)
        bottom_plane = pressure[:, :, -1]
        ghost = bottom_plane - velocity
        framed = jnp.pad(pressure, ((1, 1), (1, 1), (0, 0)))
        lateral = framed[2:, 1:-1] + framed[:-2, 1:-1] + framed[1:-1, 2:] + framed[1:-1, :-2]
        below = jnp.concatenate([pressure[:, :, 1:], ghost[:, :, None]], axis=2)
        above = jnp.concatenate([jnp.zeros_like(pressure[:, :, :1]), pressure[:, :, :-1]], axis=2)
        pressure_new = 2.0 * pressure - pressure_old + water_coef * (lateral + below + above - 6.0 * pressure)
        pressure_old, pressure = pressure, pressure_new
        padded = jnp.pad(current, ((0, 0), (1, 1), (1, 1), (1, 1)))
        updated = 2.0 * current - previous + elastic(padded, shear_depth, bulk_depth)
        updated = updated.at[2].add(-load_factor * bottom_plane[:, :, None] * contact)
        updated = updated * solid_mask
        previous, current = current, updated
        lifted.append(from_depth(current[2]))
    stacked = jnp.stack(lifted)
    reach = jnp.pad(stacked, ((0, 0), (LAG, LAG), (0, 0), (0, 0)))
    weights = recv_field.astype(jnp.float32)

    def one_lag(offset):
        window = lax.dynamic_slice_in_dim(reach, offset, NX, 1)
        return jnp.sum(window * weights, axis=0).astype(jnp.bfloat16)

    image = lax.map(one_lag, jnp.arange(2 * LAG + 1, dtype=jnp.int32))
    return pressure, from_depth(current), image
```

```python
import jax
import jax.numpy as jnp
from jax import lax
from jax.sharding import PartitionSpec as P

LAG = 10
STEPS = 4


load_factor = 0.5


def from_partner(array, axis, bit):
    return lax.ppermute(array, axis, [(i, i ^ 1 << bit) for i in range(lax.axis_size(axis))])


def padded_2(cells, sides, width):
    for axis, dim in sides:
        count = lax.axis_size(axis)
        here = lax.axis_index(axis)
        head = lax.slice_in_dim(cells, 0, width, axis=dim)
        tail = lax.slice_in_dim(cells, cells.shape[dim] - width, cells.shape[dim], axis=dim)
        before = lax.ppermute(tail, axis, [(i, (i + 1) % count) for i in range(count)])
        after = lax.ppermute(head, axis, [((i + 1) % count, i) for i in range(count)])
        cells = jnp.concatenate(
            [
                jnp.where(here == 0, 0.0, before),
                cells,
                jnp.where(here == count - 1, 0.0, after),
            ],
            axis=dim,
        )
    return cells


def passed_along(array, axis, by):
    peers = lax.axis_size(axis)
    source = lax.axis_index(axis) - by
    moved_in = lax.ppermute(array, axis, [(i, (i + by) % peers) for i in range(peers)])
    return jnp.where((source >= 0) & (source < peers), moved_in, 0.0)


def shifted(padded, step_x, step_y, step_z):
    size_x = padded.shape[-3] - 2
    size_y = padded.shape[-2] - 2
    size_z = padded.shape[-1] - 2
    return padded[
        ...,
        1 + step_x : 1 + step_x + size_x,
        1 + step_y : 1 + step_y + size_y,
        1 + step_z : 1 + step_z + size_z,
    ]


def moved(padded, first_step, second_step):
    return shifted(
        padded,
        first_step[0] + second_step[0],
        first_step[1] + second_step[1],
        first_step[2] + second_step[2],
    )


def negated(offset):
    return (-offset[0], -offset[1], -offset[2])


def elastic(padded, shear_field, bulk_field):
    anchor = (0, 0, 0)
    unit_steps = ((1, 0, 0), (0, 1, 0), (0, 0, 1))
    centre = moved(padded, anchor, anchor)
    laplace = -6.0 * centre
    for unit_step in unit_steps:
        laplace = (
            laplace + moved(padded, unit_step, anchor) + moved(padded, negated(unit_step), anchor)
        )
    pieces = []
    for first_axis in range(3):
        running = jnp.zeros_like(centre[0])
        for second_axis in range(3):
            component = padded[second_axis]
            step_a = unit_steps[first_axis]
            step_b = unit_steps[second_axis]
            if first_axis == second_axis:
                summand = (
                    moved(component, step_a, anchor)
                    + moved(component, negated(step_a), anchor)
                    - 2.0 * moved(component, anchor, anchor)
                )
            else:
                summand = 0.25 * (
                    moved(component, step_a, step_b)
                    - moved(component, step_a, negated(step_b))
                    - moved(component, negated(step_a), step_b)
                    + moved(component, negated(step_a), negated(step_b))
                )
            running = running + summand
        pieces.append(running)
    return shear_field * laplace + bulk_field * jnp.stack(pieces)


def lag_products(reach, weights, width_x):
    windows = jnp.stack([reach[offset : offset + width_x] for offset in range(2 * LAG + 1)])
    return windows * weights[None]


def on_device(p_now, p_prev, water_coef, seafloor, u_now, u_prev, shear, bulk, recv_field):
    index_gy = lax.axis_index("gy")
    lower_half = index_gy % 2 == 1
    width_x, width_y, water_cells = p_now.shape
    solid_cells = u_now.shape[-1]
    depth_cells = jnp.arange(solid_cells, dtype=jnp.int32)
    levels = seafloor[:, :, None]
    solid_mask = jnp.where(levels >= 0, depth_cells[None, None, :] >= levels, lower_half).astype(
        jnp.float32
    )
    contact = (depth_cells[None, None, :] == levels).astype(jnp.float32)
    current = u_now * solid_mask
    previous = u_prev * solid_mask
    pressure = p_now
    pressure_old = p_prev
    image = jnp.zeros((2 * LAG + 1,) + u_now.shape[1:], jnp.float32)
    for step_index in range(STEPS):
        velocity = jnp.sum((current[2] - previous[2]) * contact, axis=-1)
        bottom_plane = pressure[:, :, -1]
        other_plane, other_speed = from_partner((bottom_plane, velocity), "gy", 0)
        framed_x = padded_2(current, (("gx", 1),), 1)
        low_row = passed_along(framed_x[:, :, -1:], "gy", 2)
        high_row = passed_along(framed_x[:, :, :1], "gy", -2)
        framed_solid = jnp.concatenate([low_row, framed_x, high_row], axis=2)
        layer = jnp.where(lower_half, framed_solid[..., 0], framed_solid[..., -1])
        arriving = from_partner(layer, "gy", 0)
        load_plane = jnp.where(
            lower_half,
            jnp.concatenate([other_plane, bottom_plane], axis=1),
            jnp.concatenate([bottom_plane, other_plane], axis=1),
        )
        column_speed = velocity + other_speed
        water_speed = jnp.where(lower_half, column_speed[:, width_y:], column_speed[:, :width_y])
        ghost = bottom_plane - water_speed
        framed = padded_2(pressure, (("gx", 0), ("gy", 1)), 1)
        lateral = framed[2:, 1:-1] + framed[:-2, 1:-1] + framed[1:-1, 2:] + framed[1:-1, :-2]
        below = jnp.concatenate([pressure[:, :, 1:], ghost[:, :, None]], axis=2)
        above = jnp.concatenate([jnp.zeros_like(pressure[:, :, :1]), pressure[:, :, :-1]], axis=2)
        pressure_new = (
            2.0 * pressure - pressure_old + water_coef * (lateral + below + above - 6.0 * pressure)
        )
        pressure_old, pressure = (pressure, pressure_new)
        upper_ghost = jnp.where(lower_half, arriving, jnp.zeros_like(arriving))
        lower_ghost = jnp.where(lower_half, jnp.zeros_like(arriving), arriving)
        padded = jnp.concatenate(
            [upper_ghost[..., None], framed_solid, lower_ghost[..., None]], axis=-1
        )
        updated = 2.0 * current - previous + elastic(padded, shear, bulk)
        updated = updated.at[2].add(-load_factor * load_plane[:, :, None] * contact)
        updated = updated * solid_mask
        previous, current = (current, updated)
        reach = padded_2(current[2], (("gx", 0),), LAG)
        image = image + lag_products(reach, recv_field[step_index].astype(jnp.float32), width_x)
    return (pressure, current, image.astype(jnp.bfloat16))


def solution(mesh):
    return jax.shard_map(
        on_device,
        mesh=mesh,
        in_specs=(
            P("gx", "gy", None),
            P("gx", "gy", None),
            P("gx", "gy", None),
            P("gx", "gy"),
            P(None, "gx", "gy", None),
            P(None, "gx", "gy", None),
            P("gx", "gy", None),
            P("gx", "gy", None),
            P(None, "gx", "gy", None),
        ),
        out_specs=(P("gx", "gy", None), P(None, "gx", "gy", None), P(None, "gx", "gy", None)),
        check_vma=False,
    )
```

```python
import jax
import jax.numpy as jnp
from jax import lax
from jax.experimental import pallas as pl
from jax.experimental.pallas import tpu as pltpu
from jax.sharding import PartitionSpec as P

LAG = 10
STEPS = 4
LOAD = 0.5
F32 = jnp.float32
XS = 16
SOLID = 40
WATER = 24
DEPTH = 128
VN_LANE = 96
PB_LANE = 112
VMEM = pl.BlockSpec(memory_space=pltpu.VMEM)
PARAMS = pltpu.CompilerParams(vmem_limit_bytes=40 * 1024 * 1024)


def iota(shape, dim):
    return lax.broadcasted_iota(jnp.int32, shape, dim)


def turned(value, shift, axis):
    return pltpu.roll(value, shift % value.shape[axis], axis)


def after_y(value):
    return turned(value, -1, 0)


def before_y(value):
    return turned(value, 1, 0)


def after_z(value, ghost):
    return jnp.where(iota(value.shape, 1) == DEPTH - 1, ghost, turned(value, -1, 1))


def before_z(value, ghost):
    return jnp.where(iota(value.shape, 1) == 0, ghost, turned(value, 1, 1))


def slot(component, x):
    return 32 * component + x + 1


def coordinates():
    gx = lax.axis_index("gx")
    gy = lax.axis_index("gy")
    return gx, gy // 2, gy % 2


def edge_plane(rows, half, solid_of, vn_of, water_of):
    lane = iota((SOLID, DEPTH), 1)
    lane_of_half = lane - half
    sub = iota((8, DEPTH), 0)
    packed = jnp.zeros((SOLID, DEPTH), F32)
    bottom = jnp.zeros((WATER, DEPTH), F32)
    lane_w = iota((WATER, DEPTH), 1)
    for x in range(XS):
        for component in range(3):
            at = slot(component, x)
            packed = jnp.where(lane_of_half == at, turned(solid_of(component, x), at + 1, 1), packed)
        packed = jnp.where(lane == VN_LANE + x, vn_of(x), packed)
        bottom = jnp.where(
            lane_w == PB_LANE + x, turned(water_of(x), PB_LANE + x + 1, 1), bottom
        )
    low = half == 0
    zero = jnp.zeros((8, DEPTH), F32)
    own0, own1, own2 = bottom[0:8], bottom[8:16], bottom[16:24]
    keep = (sub < 4) != low
    spread = jnp.concatenate(
        [
            jnp.where(low, own0, zero),
            jnp.where(low, own1, zero),
            jnp.where(low, zero, own0),
            jnp.where(low, zero, own1),
            jnp.where(keep, own2, zero),
        ],
        axis=0,
    )
    return packed + spread


def velocity_of(now, before, contact_field):
    return jnp.sum(
        jnp.where(contact_field == 1.0, now - before, 0.0), axis=1, keepdims=True
    )


def paired(first, second, swap):
    return jnp.where(swap, first, turned(second, 4, 0))


def pack_kernel(
    d_ref, un_hbm, up_hbm, s_hbm, b_hbm, pn_hbm, pp_hbm, c_hbm,
    ya_ref, yb_ref, wi_ref, wo_ref,
    un, up, s_v, b_v, pn, pp, c_v, sems,
):
    gx, block, half = coordinates()
    even = block % 2 == 0
    upper = half == 0
    copies = []
    for k, (src, dst, rows) in enumerate(
        ((un_hbm, un, 24), (up_hbm, up, 24), (s_hbm, s_v, 24), (b_hbm, b_v, 24),
         (pn_hbm, pn, 8), (pp_hbm, pp, 8), (c_hbm, c_v, 8))
    ):
        for side, start in enumerate((0, rows)):
            if k < 2:
                source = src.at[:, :, pl.ds(start, 8)]
            else:
                source = src.at[:, pl.ds(start, 8)]
            copy = pltpu.make_async_copy(source, dst.at[side], sems.at[2 * k + side])
            copy.start()
            copies.append(copy)
    for copy in copies:
        copy.wait()
    sub = iota((8, DEPTH), 0)
    low = sub < 4
    for x in range(XS):
        sides = []
        for side, rows in ((0, pl.ds(0, 8)), (1, pl.ds(24, 8))):
            d = d_ref[x, rows]
            inside = d >= 1.0
            u = [jnp.where(inside, un[side, c, x], 0.0) for c in range(3)]
            v = [jnp.where(inside, up[side, c, x], 0.0) for c in range(3)]
            spare = 3 if side == 0 else 4
            for c in range(3):
                row = c if side == 0 else 5 + c
                v[c] = jnp.where(sub == spare, turned(d, spare - row, 0), v[c])
            s = jnp.where(inside, s_v[side, x], 0.0)
            b = jnp.where(inside, b_v[side, x], 0.0)
            keep = low if side == 0 else jnp.logical_not(low)
            sides.append(
                [paired(u[0], u[1], keep), paired(u[2], v[0], keep),
                 paired(v[1], v[2], keep), paired(s, b, keep)]
            )
        for k in range(4):
            head, tail = sides[0][k], sides[1][k]
            ya_ref[k, x] = jnp.where(even, tail, head)
            yb_ref[k, x] = jnp.where(even, head, tail)

    def water(target, inner, write):
        keep = low == (upper != inner)
        for x in range(XS):
            def pick(ref, at):
                return jnp.where(upper == inner, ref[1, at], ref[0, at])

            write(target, x, paired(pick(pn, x), pick(pp, x), keep))
            if x < 8:
                write(target, XS + x, paired(pick(c_v, x), pick(c_v, x + 8), keep))

    def write(ref, at, value):
        ref[at] = value

    water(wi_ref, True, write)
    water(wo_ref, False, write)


def send_faces(solid_of, water_of, a_ref, b_ref):
    even = lax.axis_index("gx") % 2 == 0
    for c in range(3):
        head, tail = solid_of(c, 0), solid_of(c, XS - 1)
        a_ref[pl.ds(SOLID * c, SOLID)] = jnp.where(even, tail, head)
        b_ref[pl.ds(SOLID * c, SOLID)] = jnp.where(even, head, tail)
    head, tail = water_of(0), water_of(XS - 1)
    a_ref[pl.ds(3 * SOLID, WATER)] = jnp.where(even, tail, head)
    b_ref[pl.ds(3 * SOLID, WATER)] = jnp.where(even, head, tail)


def received(a_ref, b_ref, rows):
    gx = lax.axis_index("gx")
    even = gx % 2 == 0
    a, b = a_ref[rows], b_ref[rows]
    before = jnp.where(gx > 0, jnp.where(even, b, a), 0.0)
    after = jnp.where(gx < lax.axis_size("gx") - 1, jnp.where(even, a, b), 0.0)
    return before, after


def corner_kernel(edge_ref, a_ref, b_ref, out_ref):
    half = lax.axis_index("gy") % 2
    lane_of_half = iota((SOLID, DEPTH), 1) - half
    packed = edge_ref[...]
    for c in (0, 2):
        before, after = received(a_ref, b_ref, pl.ds(SOLID * c, SOLID))
        for value, x in ((before, -1), (after, XS)):
            at = slot(c, x)
            packed = jnp.where(lane_of_half == at, turned(value, at + 1, 1), packed)
    out_ref[...] = packed


def assemble_kernel(
    d_ref, un_ref, up_ref, s_ref, b_ref, pn_ref, pp_ref, c_ref, ya_ref, yb_ref, wi_ref, wo_ref,
    u_out, v_out, s_out, b_out, d_out, p_out, q_out, c_out, edge_out, xa_out, xb_out,
):
    gx, block, half = coordinates()
    even = block % 2 == 0
    sub = iota((8, DEPTH), 0)
    low = sub < 4
    has_before = block > 0
    has_after = block < lax.axis_size("gy") // 2 - 1
    outer = jnp.where(half == 0, has_before, has_after)
    own, beyond = pl.ds(0, 32), pl.ds(32, 8)
    for x in range(XS):
        d = d_ref[x]
        inside = d >= 1.0
        for c in range(3):
            u_out[c, x, own] = jnp.where(inside, un_ref[c, x], 0.0)
            v_out[c, x, own] = jnp.where(inside, up_ref[c, x], 0.0)
        s_out[x, own] = jnp.where(inside, s_ref[x], 0.0)
        b_out[x, own] = jnp.where(inside, b_ref[x], 0.0)
        d_out[x, own] = d
        halo = []
        for k in range(4):
            got_a, got_b = ya_ref[k, x], yb_ref[k, x]
            from_before = jnp.where(has_before, jnp.where(even, got_b, got_a), 0.0)
            from_after = jnp.where(has_after, jnp.where(even, got_a, got_b), 0.0)
            halo.append(jnp.where(low, from_after, from_before))
            halo.append(turned(jnp.where(low, from_before, from_after), 4, 0))
        contact_rows = jnp.zeros((8, DEPTH), F32)
        for c in range(3):
            v = halo[3 + c]
            contact_rows = jnp.where(sub == c, turned(v, c - 3, 0), contact_rows)
            contact_rows = jnp.where(sub == 5 + c, turned(v, 1 + c, 0), contact_rows)
        halo.append(contact_rows)
        for c in range(3):
            u_out[c, x, beyond] = halo[c]
            v_out[c, x, beyond] = halo[3 + c]
        s_out[x, beyond] = halo[6]
        b_out[x, beyond] = halo[7]
        d_out[x, beyond] = halo[8]
        from_partner = low == (half == 0)

        def water_halo(at, natural):
            inner, beyond_it = wi_ref[at], jnp.where(outer, wo_ref[at], 0.0)
            if not natural:
                inner, beyond_it = turned(inner, 4, 0), turned(beyond_it, 4, 0)
            return jnp.where(from_partner, inner, beyond_it)

        for ref, out, at, natural in (
            (pn_ref, p_out, x, True), (pp_ref, q_out, x, False), (c_ref, c_out, XS + x % 8, x < 8)
        ):
            out[x, pl.ds(0, 16)] = ref[x]
            out[x, pl.ds(16, 8)] = water_halo(at, natural)
    edge_out[...] = edge_plane(
        None,
        half,
        lambda c, x: u_out[c, x],
        lambda x: velocity_of(u_out[2, x], v_out[2, x], d_out[x]),
        lambda x: p_out[x],
    )
    send_faces(lambda c, x: u_out[c, x], lambda x: p_out[x], xa_out, xb_out)


def step_kernel(
    last, lags,
    u_ref, v_ref, s_ref, b_ref, d_ref, p_ref, q_ref, c_ref, edge_ref,
    xa_ref, xb_ref, edge_in,
    u_out, p_out, *more,
):
    gx, block, half = coordinates()
    low_half = half == 0
    shape = (SOLID, DEPTH)
    lane = iota(shape, 1)
    at_edge = lane == jnp.where(low_half, DEPTH - 1, 0)
    sub = iota((8, DEPTH), 0)
    partner = edge_in[...]
    both = partner + edge_ref[...]
    ghosts_here = turned_by(partner, 2 * half)

    def ghost(c, x):
        return jnp.where(at_edge, turned(ghosts_here, 126 - slot(c, x), 1), 0.0)

    faces = [received(xa_ref, xb_ref, pl.ds(SOLID * c, SOLID)) for c in range(3)]
    faces.append(received(xa_ref, xb_ref, pl.ds(3 * SOLID, WATER)))

    def solid(c, x):
        if x < 0:
            return faces[c][0]
        if x >= XS:
            return faces[c][1]
        return u_ref[c, x]

    def water(x):
        if x < 0:
            return faces[3][0]
        if x >= XS:
            return faces[3][1]
        return p_ref[x]

    def plane(x):
        uy, uz = solid(1, x), solid(2, x)
        gz = ghost(2, x)
        up, down = after_y(uy), before_y(uy)
        deep, shallow = after_z(uz, gz), before_z(uz, gz)
        return up - down, up + down, deep - shallow, deep + shallow

    behind = plane(-1)
    here = plane(0)
    ghost_x_behind, ghost_x_here = ghost(0, -1), ghost(0, 0)
    for x in range(XS):
        ahead = plane(x + 1)
        ghost_x_ahead = ghost(0, x + 1)
        qy, sy_y, qz, sz_z = here
        now = [solid(c, x) for c in range(3)]
        nxt = [solid(c, x + 1) for c in range(3)]
        prv = [solid(c, x - 1) for c in range(3)]
        qx = nxt[0] - prv[0]
        sum_x = [nxt[c] + prv[c] for c in range(3)]
        dx = (ahead[0] + ahead[2]) - (behind[0] + behind[2])
        wy = qx + qz
        dy = after_y(wy) - before_y(wy)
        gy_here = ghost(1, x)
        wz = qx + qy
        ghost_wz = (ghost_x_ahead - ghost_x_behind) + (after_y(gy_here) - before_y(gy_here))
        dz = after_z(wz, ghost_wz) - before_z(wz, ghost_wz)
        sum_y = [after_y(now[0]) + before_y(now[0]), sy_y, after_y(now[2]) + before_y(now[2])]
        sum_z = [
            after_z(now[0], ghost_x_here) + before_z(now[0], ghost_x_here),
            after_z(now[1], gy_here) + before_z(now[1], gy_here),
            sz_z,
        ]
        own_sums = [sum_x[0], sum_y[1], sum_z[2]]
        mixed = [dx, dy, dz]
        s, b = s_ref[x], b_ref[x]
        d = d_ref[x]
        contact = d == 1.0
        pb = jnp.broadcast_to(both[:, PB_LANE + x : PB_LANE + x + 1], shape)
        vn = jnp.broadcast_to(both[:, VN_LANE + x : VN_LANE + x + 1], shape)
        for c in range(3):
            u = now[c]
            two = u + u
            laplace = (sum_x[c] + sum_y[c] + sum_z[c]) - 6.0 * u
            grad = (own_sums[c] - two) + 0.25 * mixed[c]
            new = (two - v_ref[c, x]) + s * laplace + b * grad
            if c == 2:
                new = new - jnp.where(contact, LOAD * pb, 0.0)
            if last:
                u_out[c, x] = new[0:32]
            else:
                u_out[c, x] = new
        beyond = jnp.where(
            sub < 4,
            jnp.where(low_half, vn[16:24], vn[32:40]),
            jnp.where(low_half, vn[32:40], vn[8:16]),
        )
        vn_water = jnp.concatenate([jnp.where(low_half, vn[0:16], vn[16:32]), beyond], axis=0)
        p = water(x)
        lateral = water(x + 1) + water(x - 1) + after_y(p) + before_y(p)
        vertical = after_z(p, p - vn_water) + before_z(p, 0.0)
        p_new = (2.0 * p - q_ref[x]) + c_ref[x] * (lateral + vertical - 6.0 * p)
        if last:
            p_out[x] = p_new[0:16]
        else:
            p_out[x] = p_new
        behind, here = here, ahead
        ghost_x_behind, ghost_x_here = ghost_x_here, ghost_x_ahead
    if lags:
        lag_a, lag_b = more[-2:]
        even = gx % 2 == 0
        for n, ref in enumerate((u_ref, u_out)[2 - lags :]):
            for k in range(LAG):
                head = ref[2, k, pl.ds(0, 32)]
                tail = ref[2, k + XS - LAG, pl.ds(0, 32)]
                lag_a[n, k] = jnp.where(even, tail, head)
                lag_b[n, k] = jnp.where(even, head, tail)
    if not last:
        edge_out, xa_out, xb_out = more[:3]
        edge_out[...] = edge_plane(
            None,
            half,
            lambda c, x: u_out[c, x],
            lambda x: velocity_of(u_out[2, x], u_ref[2, x], d_ref[x]),
            lambda x: p_out[x],
        )
        send_faces(lambda c, x: u_out[c, x], lambda x: p_out[x], xa_out, xb_out)


def turned_by(value, amount):
    return jnp.where(amount > 0, turned(value, 2, 1), value)


def image_kernel(chunk, *refs):
    u_refs, lag_refs = refs[0:4], refs[4:10]
    recv_ref, out_ref, reach = refs[10], refs[11], refs[12]
    step = pl.program_id(0)

    @pl.when(step == 0)
    def _():
        gx = lax.axis_index("gx")
        even = gx % 2 == 0
        has_before = gx > 0
        has_after = gx < lax.axis_size("gx") - 1
        t = 0
        for at in range(3):
            a_ref, b_ref = lag_refs[2 * at], lag_refs[2 * at + 1]
            for n in range(a_ref.shape[0]):
                for k in range(LAG):
                    a, b = a_ref[n, k], b_ref[n, k]
                    reach[t, k] = jnp.where(has_before, jnp.where(even, b, a), 0.0)
                    reach[t, LAG + XS + k] = jnp.where(has_after, jnp.where(even, a, b), 0.0)
                t += 1
        for t in range(STEPS):
            for x in range(XS):
                reach[t, LAG + x] = u_refs[t][2, x, pl.ds(0, 32)]

    for k in range(chunk):
        for row in (0, 16):
            rows = pl.ds(row, 16)
            weights = [recv_ref[t, k, rows].astype(F32) for t in range(STEPS)]
            for lag in range(2 * LAG + 1):
                at = step * chunk + (k + lag)
                total = reach[0, at, rows] * weights[0]
                for t in range(1, STEPS):
                    total = total + reach[t, at, rows] * weights[t]
                out_ref[lag, k, rows] = total.astype(jnp.bfloat16)


def call(body, outs, *args, specs=None, scratch=()):
    return pl.pallas_call(
        body,
        out_shape=[jax.ShapeDtypeStruct(shape, F32) for shape in outs],
        in_specs=specs or [VMEM] * len(args),
        out_specs=[VMEM] * len(outs),
        scratch_shapes=list(scratch),
        compiler_params=PARAMS,
    )(*args)


def swapped(size, width):
    return [(i, i ^ width) for i in range(size)]


def crossed(size, width):
    return [(i, (((i + width) % size ^ width) - width) % size) for i in range(size)]


def on_device(p_now, p_prev, water_coef, seafloor, u_now, u_prev, shear, bulk, recv_field):
    size_x = lax.axis_size("gx")
    size_y = lax.axis_size("gy")
    half = lax.axis_index("gy") % 2
    far = jnp.where(half == 0, 4 * DEPTH, -4 * DEPTH)
    levels = jnp.where(seafloor >= 0, seafloor, far)[:, :, None]
    depth = jnp.arange(1, DEPTH + 1, dtype=jnp.int32)[None, None, :]
    field = (depth - levels).astype(F32)
    raw = (field, u_now, u_prev, shear, bulk, p_now, p_prev, water_coef)
    tile = (XS, 8, DEPTH)
    y_payload = (4,) + tile
    w_payload = (XS + XS // 2, 8, DEPTH)
    hbm = pl.BlockSpec(memory_space=pltpu.HBM)
    ya, yb, w_in, w_out = call(
        pack_kernel,
        [y_payload, y_payload, w_payload, w_payload],
        *raw,
        specs=[VMEM] + [hbm] * 7,
        scratch=[pltpu.VMEM((2, 3) + tile, F32)] * 2
        + [pltpu.VMEM((2,) + tile, F32)] * 5
        + [pltpu.SemaphoreType.DMA((14,))],
    )
    ya = lax.ppermute(ya, "gy", swapped(size_y, 2))
    yb = lax.ppermute(yb, "gy", crossed(size_y, 2))
    w_out = lax.ppermute(w_out, "gy", crossed(size_y, 1))
    w_in = lax.ppermute(w_in, "gy", swapped(size_y, 1))
    solid = (XS, SOLID, DEPTH)
    water = (XS, WATER, DEPTH)
    face = (3 * SOLID + WATER, DEPTH)
    plane = (SOLID, DEPTH)
    u, v, s, b, d, p, q, c, edge, xa, xb = call(
        assemble_kernel,
        [(3,) + solid, (3,) + solid, solid, solid, solid, water, water, water, plane, face, face],
        *raw, ya, yb, w_in, w_out,
    )
    verticals, reaches = [], []
    for t in range(STEPS):
        last = t == STEPS - 1
        lags = (0, 2, 1, 1)[t]
        xa = lax.ppermute(xa, "gx", swapped(size_x, 1))
        xb = lax.ppermute(xb, "gx", crossed(size_x, 1))
        edge_full, = call(corner_kernel, [plane], edge, xa, xb)
        edge_in = lax.ppermute(edge_full, "gy", swapped(size_y, 1))
        if last:
            outs = [(3, XS, 32, DEPTH), (XS, 16, DEPTH)]
        else:
            outs = [(3,) + solid, water, plane, face, face]
        outs = outs + [(lags, LAG, 32, DEPTH)] * (2 if lags else 0)

        def body(*refs, last=last, lags=lags):
            step_kernel(last, lags, *refs)

        u_new, p_new, *more = call(body, outs, u, v, s, b, d, p, q, c, edge, xa, xb, edge_in)
        v, u, q, p = u, u_new, p, p_new
        if not last:
            edge, xa, xb = more[:3]
        if lags:
            reaches.append(lax.ppermute(more[-2], "gx", swapped(size_x, 1)))
            reaches.append(lax.ppermute(more[-1], "gx", crossed(size_x, 1)))
        verticals.append(u)
    chunk = 4

    def image_body(*refs):
        image_kernel(chunk, *refs)

    image = pl.pallas_call(
        image_body,
        out_shape=jax.ShapeDtypeStruct((2 * LAG + 1, XS, 32, DEPTH), jnp.bfloat16),
        grid=(XS // chunk,),
        in_specs=[VMEM] * 10 + [pl.BlockSpec((STEPS, chunk, 32, DEPTH), lambda i: (0, i, 0, 0))],
        out_specs=pl.BlockSpec((2 * LAG + 1, chunk, 32, DEPTH), lambda i: (0, i, 0, 0)),
        scratch_shapes=[pltpu.VMEM((STEPS, XS + 2 * LAG, 32, DEPTH), F32)],
        compiler_params=PARAMS,
    )(*verticals, *reaches, recv_field)
    return (p, u, image)


def solution(mesh):
    return jax.shard_map(
        on_device,
        mesh=mesh,
        in_specs=(
            P("gx", "gy", None),
            P("gx", "gy", None),
            P("gx", "gy", None),
            P("gx", "gy"),
            P(None, "gx", "gy", None),
            P(None, "gx", "gy", None),
            P("gx", "gy", None),
            P("gx", "gy", None),
            P(None, "gx", "gy", None),
        ),
        out_specs=(P("gx", "gy", None), P(None, "gx", "gy", None), P(None, "gx", "gy", None)),
        check_vma=False,
    )
```

```python
import jax
import jax.numpy as jnp
from jax import lax
from jax.experimental import pallas as pl
from jax.experimental.pallas import tpu as pltpu
from jax.sharding import PartitionSpec as P

LAG = 10
STEPS = 4
LOAD = 0.5
F32 = jnp.float32
XS = 16
SOLID = 40
WATER = 24
DEPTH = 128
FACE = 3 * SOLID + WATER
OWN = 32
INNER = 192
VMEM = pl.BlockSpec(memory_space=pltpu.VMEM)
PACK_LIMIT = 50
PARAMS = pltpu.CompilerParams(vmem_limit_bytes=40 * 1024 * 1024)


def iota(shape, dim):
    return lax.broadcasted_iota(jnp.int32, shape, dim)


def turned(value, shift, axis):
    return pltpu.roll(value, shift % value.shape[axis], axis)


def after_y(value):
    return turned(value, -1, 0)


def before_y(value):
    return turned(value, 1, 0)


def after_z(value, ghost):
    return jnp.where(iota(value.shape, 1) == DEPTH - 1, ghost, turned(value, -1, 1))


def before_z(value, ghost):
    return jnp.where(iota(value.shape, 1) == 0, ghost, turned(value, 1, 1))


def coordinates():
    gx = lax.axis_index("gx")
    gy = lax.axis_index("gy")
    return gx, gy // 2, gy % 2


def coupling(half, vn_of, water_of):
    group = iota((SOLID, DEPTH), 1) // 8
    group_w = iota((WATER, DEPTH), 1) // 8
    sub = iota((8, DEPTH), 0)
    velocity = jnp.zeros((SOLID, DEPTH), F32)
    bottom = jnp.zeros((WATER, DEPTH), F32)
    for x in range(XS):
        velocity = jnp.where(group == x, vn_of(x), velocity)
        bottom = jnp.where(group_w == x, water_of(x)[:, DEPTH - 1 : DEPTH], bottom)
    low = half == 0
    zero = jnp.zeros((8, DEPTH), F32)
    own0, own1, own2 = bottom[0:8], bottom[8:16], bottom[16:24]
    keep = (sub < 4) != low
    spread = jnp.concatenate(
        [
            jnp.where(low, own0, zero),
            jnp.where(low, own1, zero),
            jnp.where(low, zero, own0),
            jnp.where(low, zero, own1),
            jnp.where(keep, own2, zero),
        ],
        axis=0,
    )
    return spread, velocity


def own_strip(half, plane_of):
    lane = iota((OWN, DEPTH), 1)
    group = lane // 8
    strip = jnp.zeros((OWN, DEPTH), F32)
    for x in range(XS):
        strip = jnp.where(group == x, turned(plane_of(x), 8 * x + 4, 1), strip)
    return jnp.where((lane % 8 < 4) == (half == 0), strip, 0.0)


def send_strip_faces(strips, a_ref, b_ref, rows):
    even = lax.axis_index("gx") % 2 == 0
    group = iota((SOLID, DEPTH), 1) // 8
    head = tail = jnp.zeros((SOLID, DEPTH), F32)
    for c in range(3):
        head = jnp.where(group == c, turned(strips[c], 8 * c, 1), head)
        tail = jnp.where(group == c, turned(strips[c], 8 * c + 8, 1), tail)
    a_ref[rows] = jnp.where(even, tail, head)
    b_ref[rows] = jnp.where(even, head, tail)


def strip_step(now, old, s, b, contact, pb, before, after):
    lane = iota((SOLID, DEPTH), 1)

    def next_x(value, face):
        return jnp.where(lane >= DEPTH - 8, turned(face, DEPTH - 8, 1), turned(value, -8, 1))

    def prev_x(value, face):
        return jnp.where(lane < 8, face, turned(value, 8, 1))

    def next_z(value):
        return turned(value, -1, 1)

    def prev_z(value):
        return turned(value, 1, 1)

    def x_weight(u1, u2):
        return (after_y(u1) - before_y(u1)) + (next_z(u2) - prev_z(u2))

    shifts = []
    for c in range(3):
        u = now[c]
        shifts.append((
            (next_x(u, after[c]), prev_x(u, before[c])),
            (after_y(u), before_y(u)),
            (next_z(u), prev_z(u)),
        ))
    q = [shifts[c][c][0] - shifts[c][c][1] for c in range(3)]
    wx, wy, wz = q[1] + q[2], q[0] + q[2], q[0] + q[1]
    mixed = [
        next_x(wx, x_weight(after[1], after[2])) - prev_x(wx, x_weight(before[1], before[2])),
        after_y(wy) - before_y(wy),
        next_z(wz) - prev_z(wz),
    ]
    new = []
    for c in range(3):
        u = now[c]
        two = u + u
        sums = [up + down for up, down in shifts[c]]
        laplace = (sums[0] + sums[1] + sums[2]) - 6.0 * u
        grad = (sums[c] - two) + 0.25 * mixed[c]
        value = (two - old[c]) + s * laplace + b * grad
        if c == 2:
            value = value - jnp.where(contact, LOAD * pb, 0.0)
        new.append(value)
    return new


def velocity_of(now, before, contact_field):
    return jnp.sum(
        jnp.where(contact_field == 1.0, now - before, 0.0), axis=1, keepdims=True
    )


def paired(first, second, swap):
    return jnp.where(swap, first, turned(second, 4, 0))


def pack_kernel(
    d_ref, un_hbm, up_hbm, elastic, pressures,
    un, up, s_v, b_v, ya_ref, yb_ref, wo_ref, partner_ref, sems,
):
    gx, block, half = coordinates()
    even = block % 2 == 0
    upper = half == 0
    copies = []
    for k, (src, dst) in enumerate(
        ((un_hbm, un), (up_hbm, up))
    ):
        copy = pltpu.make_async_copy(src, dst, sems.at[k])
        copy.start()
        copies.append(copy)
    for copy in copies:
        copy.wait()
    pn, pp, c_v = (pressures.at[k] for k in range(3))
    sub = iota((8, DEPTH), 0)
    low = sub < 4
    for x in range(XS):
        inside = d_ref[x] >= 1.0
        for ref in (un, up):
            for c in range(3):
                ref[c, x] = jnp.where(inside, ref[c, x], 0.0)
        s_v[x] = jnp.where(inside, elastic[0, x], 0.0)
        b_v[x] = jnp.where(inside, elastic[1, x], 0.0)
        sides = []
        for side, rows in ((0, pl.ds(0, 8)), (1, pl.ds(24, 8))):
            d = d_ref[x, rows]
            u = [un[c, x, rows] for c in range(3)]
            v = [up[c, x, rows] for c in range(3)]
            spare = 3 if side == 0 else 4
            for c in range(3):
                row = c if side == 0 else 5 + c
                v[c] = jnp.where(sub == spare, turned(d, spare - row, 0), v[c])
            keep = low if side == 0 else jnp.logical_not(low)
            sides.append(
                [paired(u[0], u[1], keep), paired(u[2], v[0], keep),
                 paired(v[1], v[2], keep), paired(s_v[x, rows], b_v[x, rows], keep)]
            )
        for k in range(4):
            head, tail = sides[0][k], sides[1][k]
            ya_ref[k, x] = jnp.where(even, tail, head)
            yb_ref[k, x] = jnp.where(even, head, tail)
    for inner in (True, False):
        keep = low == (upper != inner)

        def pick(ref, at):
            return jnp.where(upper == inner, ref[at, pl.ds(8, 8)], ref[at, pl.ds(0, 8)])

        tiles = [paired(pick(pn, x), pick(pp, x), keep) for x in range(XS)]
        tiles += [paired(pick(c_v, x), pick(c_v, x + 8), keep) for x in range(8)]
        for at, tile in enumerate(tiles):
            if inner:
                partner_ref[pl.ds(8 * at, 8)] = tile
            else:
                wo_ref[at] = tile
    planes = [lambda x, c=c: un[c, x] for c in range(3)]
    planes += [lambda x, c=c: up[c, x] for c in range(3)]
    planes += [lambda x: s_v[x], lambda x: b_v[x], lambda x: d_ref[x]]
    for k, plane_of in enumerate(planes):
        partner_ref[pl.ds(INNER + OWN * k, OWN)] = own_strip(half, plane_of)


def strip_kernel(own_ref, got_ref, full_ref, ya_ref, yb_ref):
    gx, block, half = coordinates()
    even = block % 2 == 0
    low = iota((8, DEPTH), 0) < 4
    full_ref[...] = own_ref[pl.ds(INNER, 9 * OWN)] + got_ref[pl.ds(INNER, 9 * OWN)]
    for pair in range(5):
        first, second = 2 * pair, min(2 * pair + 1, 8)
        sides = []
        for row, keep in ((0, low), (OWN - 8, jnp.logical_not(low))):
            sides.append(
                paired(full_ref[pl.ds(OWN * first + row, 8)], full_ref[pl.ds(OWN * second + row, 8)], keep)
            )
        ya_ref[pl.ds(8 * pair, 8)] = jnp.where(even, sides[1], sides[0])
        yb_ref[pl.ds(8 * pair, 8)] = jnp.where(even, sides[0], sides[1])


def send_faces(solid_of, water_of, a_ref, b_ref):
    even = lax.axis_index("gx") % 2 == 0
    for c in range(3):
        head, tail = solid_of(c, 0), solid_of(c, XS - 1)
        a_ref[pl.ds(SOLID * c, SOLID)] = jnp.where(even, tail, head)
        b_ref[pl.ds(SOLID * c, SOLID)] = jnp.where(even, head, tail)
    head, tail = water_of(0), water_of(XS - 1)
    a_ref[pl.ds(3 * SOLID, WATER)] = jnp.where(even, tail, head)
    b_ref[pl.ds(3 * SOLID, WATER)] = jnp.where(even, head, tail)


def received(a_ref, b_ref, rows):
    gx = lax.axis_index("gx")
    even = gx % 2 == 0
    a, b = a_ref[rows], b_ref[rows]
    before = jnp.where(gx > 0, jnp.where(even, b, a), 0.0)
    after = jnp.where(gx < lax.axis_size("gx") - 1, jnp.where(even, a, b), 0.0)
    return before, after


def assemble_kernel(
    d_ref, un_ref, up_ref, s_ref, b_ref, pressures,
    ya_ref, yb_ref, wo_ref, partner_ref, full_ref, ysa_ref, ysb_ref,
    u_out, v_out, s_out, b_out, d_out, p_out, q_out, c_out, now_out, old_out, static_out, coupling_out, xa_out, xb_out,
):
    gx, block, half = coordinates()
    even = block % 2 == 0
    sub = iota((8, DEPTH), 0)
    low = sub < 4
    has_before = block > 0
    has_after = block < lax.axis_size("gy") // 2 - 1
    outer = jnp.where(half == 0, has_before, has_after)
    own, beyond = pl.ds(0, OWN), pl.ds(OWN, 8)

    def halos(got_a, got_b):
        from_before = jnp.where(has_before, jnp.where(even, got_b, got_a), 0.0)
        from_after = jnp.where(has_after, jnp.where(even, got_a, got_b), 0.0)
        return (
            jnp.where(low, from_after, from_before),
            turned(jnp.where(low, from_before, from_after), 4, 0),
        )

    strip_halos = []
    for pair in range(5):
        rows = pl.ds(8 * pair, 8)
        strip_halos.extend(halos(ysa_ref[rows], ysb_ref[rows]))
    for k in range(9):
        ref = (now_out, old_out, static_out)[k // 3]
        ref[pl.ds(SOLID * (k % 3), OWN)] = full_ref[pl.ds(OWN * k, OWN)]
        ref[pl.ds(SOLID * (k % 3) + OWN, 8)] = strip_halos[k]
    for x in range(XS):
        for c in range(3):
            u_out[c, x, own] = un_ref[c, x]
            v_out[c, x, own] = up_ref[c, x]
        s_out[x, own] = s_ref[x]
        b_out[x, own] = b_ref[x]
        d_out[x, own] = d_ref[x]
        halo = []
        for k in range(4):
            halo.extend(halos(ya_ref[k, x], yb_ref[k, x]))
        contact_rows = jnp.zeros((8, DEPTH), F32)
        for c in range(3):
            v = halo[3 + c]
            contact_rows = jnp.where(sub == c, turned(v, c - 3, 0), contact_rows)
            contact_rows = jnp.where(sub == 5 + c, turned(v, 1 + c, 0), contact_rows)
        halo.append(contact_rows)
        for c in range(3):
            u_out[c, x, beyond] = halo[c]
            v_out[c, x, beyond] = halo[3 + c]
        s_out[x, beyond] = halo[6]
        b_out[x, beyond] = halo[7]
        d_out[x, beyond] = halo[8]
        pn_ref, pp_ref, c_ref = (pressures.at[k] for k in range(3))
        from_partner = low == (half == 0)

        def water_halo(at, natural):
            inner, beyond_it = partner_ref[pl.ds(8 * at, 8)], jnp.where(outer, wo_ref[at], 0.0)
            if not natural:
                inner, beyond_it = turned(inner, 4, 0), turned(beyond_it, 4, 0)
            return jnp.where(from_partner, inner, beyond_it)

        for ref, out, at, natural in (
            (pn_ref, p_out, x, True), (pp_ref, q_out, x, False), (c_ref, c_out, XS + x % 8, x < 8)
        ):
            out[x, pl.ds(0, 16)] = ref[x]
            out[x, pl.ds(16, 8)] = water_halo(at, natural)
    bottom, velocity = coupling(
        half,
        lambda x: velocity_of(u_out[2, x], v_out[2, x], d_out[x]),
        lambda x: p_out[x],
    )
    coupling_out[pl.ds(0, SOLID)] = bottom
    coupling_out[pl.ds(SOLID, SOLID)] = velocity
    strips = [now_out[pl.ds(SOLID * c, SOLID)] for c in range(3)]
    send_strip_faces(strips, xa_out, xb_out, pl.ds(FACE, SOLID))
    send_faces(lambda c, x: u_out[c, x], lambda x: p_out[x], xa_out, xb_out)


def step_kernel(last, lags, *refs):
    u_ref, v_ref, s_ref, b_ref, d_ref, p_ref, q_ref, c_ref = refs[0:8]
    now_ref, old_ref, static_ref, own_ref, got_ref, xa_ref, xb_ref = refs[8:15]
    strip_rows = pl.ds(FACE, SOLID)
    u_out, p_out = refs[15:17]
    more = refs[17:]
    gx, block, half = coordinates()
    low_half = half == 0
    shape = (SOLID, DEPTH)
    lane = iota(shape, 1)
    at_edge = lane == jnp.where(low_half, DEPTH - 1, 0)
    sub = iota((8, DEPTH), 0)
    bottom = own_ref[pl.ds(0, SOLID)] + got_ref[pl.ds(0, SOLID)]
    velocity = own_ref[pl.ds(SOLID, SOLID)] + got_ref[pl.ds(SOLID, SOLID)]
    strips = [now_ref[pl.ds(SOLID * c, SOLID)] for c in range(3)]
    strip_before, strip_after = [], []
    for value, out in zip(received(xa_ref, xb_ref, strip_rows), (strip_before, strip_after)):
        out.extend(turned(value, -8 * c, 1) if c else value for c in range(3))

    def of_half(value):
        return jnp.where(low_half, value, turned(value, 2, 1))

    ghosts = [[of_half(v) for v in group] for group in (strip_before, strips, strip_after)]

    def ghost(c, x):
        if x < 0:
            source, shift = ghosts[0][c], 123
        elif x >= XS:
            source, shift = ghosts[2][c], 123
        else:
            source, shift = ghosts[1][c], 123 - 8 * x
        return jnp.where(at_edge, turned(source, shift, 1), 0.0)

    faces = [received(xa_ref, xb_ref, pl.ds(SOLID * c, SOLID)) for c in range(3)]
    faces.append(received(xa_ref, xb_ref, pl.ds(3 * SOLID, WATER)))

    def solid(c, x):
        if x < 0:
            return faces[c][0]
        if x >= XS:
            return faces[c][1]
        return u_ref[c, x]

    def water(x):
        if x < 0:
            return faces[3][0]
        if x >= XS:
            return faces[3][1]
        return p_ref[x]

    def plane(x):
        uy, uz = solid(1, x), solid(2, x)
        gz = ghost(2, x)
        up, down = after_y(uy), before_y(uy)
        deep, shallow = after_z(uz, gz), before_z(uz, gz)
        return up - down, up + down, deep - shallow, deep + shallow

    behind = plane(-1)
    here = plane(0)
    ghost_x_behind, ghost_x_here = ghost(0, -1), ghost(0, 0)
    for x in range(XS):
        ahead = plane(x + 1)
        ghost_x_ahead = ghost(0, x + 1)
        qy, sy_y, qz, sz_z = here
        now = [solid(c, x) for c in range(3)]
        nxt = [solid(c, x + 1) for c in range(3)]
        prv = [solid(c, x - 1) for c in range(3)]
        qx = nxt[0] - prv[0]
        sum_x = [nxt[c] + prv[c] for c in range(3)]
        dx = (ahead[0] + ahead[2]) - (behind[0] + behind[2])
        wy = qx + qz
        dy = after_y(wy) - before_y(wy)
        gy_here = ghost(1, x)
        wz = qx + qy
        ghost_wz = (ghost_x_ahead - ghost_x_behind) + (after_y(gy_here) - before_y(gy_here))
        dz = after_z(wz, ghost_wz) - before_z(wz, ghost_wz)
        sum_y = [after_y(now[0]) + before_y(now[0]), sy_y, after_y(now[2]) + before_y(now[2])]
        sum_z = [
            after_z(now[0], ghost_x_here) + before_z(now[0], ghost_x_here),
            after_z(now[1], gy_here) + before_z(now[1], gy_here),
            sz_z,
        ]
        own_sums = [sum_x[0], sum_y[1], sum_z[2]]
        mixed = [dx, dy, dz]
        s, b = s_ref[x], b_ref[x]
        d = d_ref[x]
        contact = d == 1.0
        pb = jnp.broadcast_to(bottom[:, 8 * x : 8 * x + 1], shape)
        vn = jnp.broadcast_to(velocity[:, 8 * x : 8 * x + 1], shape)
        for c in range(3):
            u = now[c]
            two = u + u
            laplace = (sum_x[c] + sum_y[c] + sum_z[c]) - 6.0 * u
            grad = (own_sums[c] - two) + 0.25 * mixed[c]
            new = (two - v_ref[c, x]) + s * laplace + b * grad
            if c == 2:
                new = new - jnp.where(contact, LOAD * pb, 0.0)
            if last:
                u_out[c, x] = new[0:32]
            else:
                u_out[c, x] = new
        beyond = jnp.where(
            sub < 4,
            jnp.where(low_half, vn[16:24], vn[32:40]),
            jnp.where(low_half, vn[32:40], vn[8:16]),
        )
        vn_water = jnp.concatenate([jnp.where(low_half, vn[0:16], vn[16:32]), beyond], axis=0)
        p = water(x)
        lateral = water(x + 1) + water(x - 1) + after_y(p) + before_y(p)
        vertical = after_z(p, p - vn_water) + before_z(p, 0.0)
        p_new = (2.0 * p - q_ref[x]) + c_ref[x] * (lateral + vertical - 6.0 * p)
        if last:
            p_out[x] = p_new[0:16]
        else:
            p_out[x] = p_new
        behind, here = here, ahead
        ghost_x_behind, ghost_x_here = ghost_x_here, ghost_x_ahead
    if lags:
        lag_a, lag_b = more[-2:]
        even = gx % 2 == 0
        for n, ref in enumerate((u_ref, u_out)[2 - lags :]):
            for k in range(LAG):
                head = ref[2, k, pl.ds(0, 32)]
                tail = ref[2, k + XS - LAG, pl.ds(0, 32)]
                lag_a[n, k] = jnp.where(even, tail, head)
                lag_b[n, k] = jnp.where(even, head, tail)
    if last:
        for x in range(XS):
            more[0][x] = u_out[2, x]
        return
    strip_out, coupling_out, xa_out, xb_out = more[:4]
    static = [static_ref[pl.ds(SOLID * k, SOLID)] for k in range(3)]
    old = [old_ref[pl.ds(SOLID * c, SOLID)] for c in range(3)]
    strips = strip_step(
        strips, old, static[0], static[1], static[2] == 1.0, bottom, strip_before, strip_after
    )
    for c in range(3):
        strip_out[pl.ds(SOLID * c, SOLID)] = strips[c]
    send_strip_faces(strips, xa_out, xb_out, pl.ds(FACE, SOLID))
    send_faces(lambda c, x: u_out[c, x], lambda x: p_out[x], xa_out, xb_out)
    bottom, velocity = coupling(
        half,
        lambda x: velocity_of(u_out[2, x], u_ref[2, x], d_ref[x]),
        lambda x: p_out[x],
    )
    coupling_out[pl.ds(0, SOLID)] = bottom
    coupling_out[pl.ds(SOLID, SOLID)] = velocity


def own_range(lag):
    return max(0, LAG - lag), min(XS, XS + LAG - lag)


def open_pairs():
    pairs = []
    for lag in range(2 * LAG + 1):
        low, high = own_range(lag)
        pairs.extend((lag, x) for x in range(XS) if not low <= x < high)
    return {pair: at for at, pair in enumerate(pairs)}


def lag_halos(a, b):
    gx = lax.axis_index("gx")
    even = gx % 2 == 0
    before = jnp.where(gx > 0, jnp.where(even, b, a), 0.0)
    after = jnp.where(gx < lax.axis_size("gx") - 1, jnp.where(even, a, b), 0.0)
    return before, after


def image_kernel(
    u0, u1, u2, u3, first_a, first_b, third_a, third_b, recv_ref,
    out_hbm, open_ref, halo, weights, stage, sems,
):
    for t, (a_ref, b_ref, n) in enumerate(
        ((first_a, first_b, 0), (first_a, first_b, 1), (third_a, third_b, 0))
    ):
        for k in range(LAG):
            halo[t, k], halo[t, LAG + k] = lag_halos(a_ref[n, k], b_ref[n, k])
    for t in range(STEPS):
        for x in range(XS):
            weights[t, x] = recv_ref[t, x].astype(F32)

    def column(t, x):
        if x < 0:
            return halo[t, x + LAG]
        if x >= XS:
            return halo[t, x - XS + LAG]
        if t == STEPS - 1:
            return u3[x]
        return (u0, u1, u2)[t][2, x, pl.ds(0, OWN)]

    pairs = open_pairs()
    copies = []
    for lag in range(2 * LAG + 1):
        low, high = own_range(lag)
        for x in range(XS):
            at = x + lag - LAG
            total = column(0, at) * weights[0, x]
            total = total + column(1, at) * weights[1, x]
            total = total + column(2, at) * weights[2, x]
            if low <= x < high:
                total = total + column(3, at) * weights[3, x]
                stage[lag, x] = total.astype(jnp.bfloat16)
            else:
                open_ref[pairs[lag, x]] = total
        columns = pl.ds(low, high - low)
        copy = pltpu.make_async_copy(
            stage.at[lag, columns], out_hbm.at[lag, columns], sems.at[lag]
        )
        copy.start()
        copies.append(copy)
    for copy in copies:
        copy.wait()


def finish_kernel(open_ref, a_ref, b_ref, recv_ref, image_hbm, out_hbm, halo, stage, sems):
    for k in range(LAG):
        halo[k], halo[LAG + k] = lag_halos(a_ref[0, k], b_ref[0, k])
    pairs = open_pairs()
    copies = []
    for n, lag in enumerate(k for k in range(2 * LAG + 1) if k != LAG):
        low, high = own_range(lag)
        start, stop = (0, low) if lag < LAG else (high, XS)
        for x in range(start, stop):
            at = x + lag if lag < LAG else x + lag - XS
            total = open_ref[pairs[lag, x]] + halo[at] * recv_ref[STEPS - 1, x].astype(F32)
            stage[lag, x] = total.astype(jnp.bfloat16)
        columns = pl.ds(start, stop - start)
        copy = pltpu.make_async_copy(
            stage.at[lag, columns], out_hbm.at[lag, columns], sems.at[n]
        )
        copy.start()
        copies.append(copy)
    for copy in copies:
        copy.wait()


def call(body, outs, *args, specs=None, scratch=(), limit=40):
    return pl.pallas_call(
        body,
        out_shape=[jax.ShapeDtypeStruct(shape, F32) for shape in outs],
        in_specs=specs or [VMEM] * len(args),
        out_specs=[VMEM] * len(outs),
        scratch_shapes=list(scratch),
        compiler_params=pltpu.CompilerParams(vmem_limit_bytes=limit * 1024 * 1024),
    )(*args)


def swapped(size, width):
    return [(i, i ^ width) for i in range(size)]


def crossed(size, width):
    return [(i, (((i + width) % size ^ width) - width) % size) for i in range(size)]


def on_device(p_now, p_prev, water_coef, seafloor, u_now, u_prev, shear, bulk, recv_field):
    size_x = lax.axis_size("gx")
    size_y = lax.axis_size("gy")
    half = lax.axis_index("gy") % 2
    far = jnp.where(half == 0, 4 * DEPTH, -4 * DEPTH)
    levels = jnp.where(seafloor >= 0, seafloor, far)[:, :, None]
    depth = jnp.arange(1, DEPTH + 1, dtype=jnp.int32)[None, None, :]
    field = (depth - levels).astype(F32)
    pressures = jnp.stack([p_now, p_prev, water_coef])
    raw = (field, u_now, u_prev, jnp.stack([shear, bulk]), pressures)
    tile = (XS, 8, DEPTH)
    y_payload = (4,) + tile
    w_payload = (XS + XS // 2, 8, DEPTH)
    hbm = pl.BlockSpec(memory_space=pltpu.HBM)
    *masked, ya, yb, w_out, to_partner = call(
        pack_kernel,
        [u_now.shape, u_now.shape, shear.shape, shear.shape, y_payload, y_payload, w_payload, (INNER + 9 * OWN, DEPTH)],
        *raw,
        specs=[VMEM, hbm, hbm, VMEM, VMEM],
        scratch=[pltpu.SemaphoreType.DMA((2,))],
        limit=PACK_LIMIT,
    )

    def to_y(first, second):
        return (
            lax.ppermute(first, "gy", swapped(size_y, 2)),
            lax.ppermute(second, "gy", crossed(size_y, 2)),
        )

    partner = lax.ppermute(to_partner, "gy", swapped(size_y, 1))
    ya, yb = to_y(ya, yb)
    w_out = lax.ppermute(w_out, "gy", crossed(size_y, 1))
    y_strip = (SOLID, DEPTH)
    full, ysa, ysb = call(strip_kernel, [(9 * OWN, DEPTH), y_strip, y_strip], to_partner, partner)
    ysa, ysb = to_y(ysa, ysb)
    solid = (XS, SOLID, DEPTH)
    water = (XS, WATER, DEPTH)
    face = (FACE + SOLID, DEPTH)
    strip = (3 * SOLID, DEPTH)
    pair = (2 * SOLID, DEPTH)
    u, v, s, b, d, p, q, c, now, old, static, own, xa, xb = call(
        assemble_kernel,
        [(3,) + solid, (3,) + solid, solid, solid, solid, water, water, water,
         strip, strip, strip, pair, face, face],
        field, *masked, pressures, ya, yb, w_out, partner, full, ysa, ysb,
    )

    def to_x(first, second):
        return (
            lax.ppermute(first, "gx", swapped(size_x, 1)),
            lax.ppermute(second, "gx", crossed(size_x, 1)),
        )

    got = lax.ppermute(own, "gy", swapped(size_y, 1))
    faces = to_x(xa, xb)
    verticals, reaches = [], []
    for t in range(STEPS):
        last = t == STEPS - 1
        lags = (0, 2, 1, 1)[t]
        if last:
            outs = [(3, XS, 32, DEPTH), (XS, 16, DEPTH), (XS, 32, DEPTH)]
        else:
            outs = [(3,) + solid, water, strip, pair, face, face]
        outs = outs + [(lags, LAG, 32, DEPTH)] * (2 if lags else 0)

        def body(*refs, last=last, lags=lags):
            step_kernel(last, lags, *refs)

        u_new, p_new, *more = call(
            body, outs, u, v, s, b, d, p, q, c, now, old, static, own, got, *faces
        )
        v, u, q, p = u, u_new, p, p_new
        if last:
            verticals.append(more[0])
        else:
            verticals.append(u)
            old, now, own = now, more[0], more[1]
            faces = to_x(more[2], more[3])
            got = lax.ppermute(own, "gy", swapped(size_y, 1))
        if lags:
            reaches += to_x(more[-2], more[-1])
    lags = 2 * LAG + 1
    image_shape = jax.ShapeDtypeStruct((lags, XS, OWN, DEPTH), jnp.bfloat16)
    open_shape = jax.ShapeDtypeStruct((len(open_pairs()), OWN, DEPTH), F32)
    stage = pltpu.VMEM(image_shape.shape, jnp.bfloat16)
    image, unfinished = pl.pallas_call(
        image_kernel,
        out_shape=[image_shape, open_shape],
        in_specs=[VMEM] * 9,
        out_specs=[hbm, VMEM],
        scratch_shapes=[
            pltpu.VMEM((STEPS - 1, 2 * LAG, OWN, DEPTH), F32),
            pltpu.VMEM((STEPS, XS, OWN, DEPTH), F32),
            stage,
            pltpu.SemaphoreType.DMA((lags,)),
        ],
        compiler_params=PARAMS,
    )(*verticals, *reaches[0:4], recv_field)
    image = pl.pallas_call(
        finish_kernel,
        out_shape=image_shape,
        in_specs=[VMEM] * 4 + [hbm],
        out_specs=hbm,
        scratch_shapes=[
            pltpu.VMEM((2 * LAG, OWN, DEPTH), F32),
            stage,
            pltpu.SemaphoreType.DMA((lags - 1,)),
        ],
        input_output_aliases={4: 0},
        compiler_params=PARAMS,
    )(unfinished, *reaches[4:6], recv_field, image)
    return (p, u, image)


def solution(mesh):
    return jax.shard_map(
        on_device,
        mesh=mesh,
        in_specs=(
            P("gx", "gy", None),
            P("gx", "gy", None),
            P("gx", "gy", None),
            P("gx", "gy"),
            P(None, "gx", "gy", None),
            P(None, "gx", "gy", None),
            P("gx", "gy", None),
            P("gx", "gy", None),
            P(None, "gx", "gy", None),
        ),
        out_specs=(P("gx", "gy", None), P(None, "gx", "gy", None), P(None, "gx", "gy", None)),
        check_vma=False,
    )
```

```python
import jax
import jax.numpy as jnp
from jax import lax
from jax.experimental import pallas as pl
from jax.experimental.pallas import tpu as pltpu
from jax.sharding import PartitionSpec as P

LAG = 10
STEPS = 4
LOAD = 0.5
F32 = jnp.float32
XS = 16
SOLID = 40
WATER = 24
DEPTH = 128
FACE = 3 * SOLID + WATER
OWN = 32
INNER = 192
VMEM = pl.BlockSpec(memory_space=pltpu.VMEM)
PACK_LIMIT = 49.5
PARAMS = pltpu.CompilerParams(vmem_limit_bytes=40 * 1024 * 1024)


def iota(shape, dim):
    return lax.broadcasted_iota(jnp.int32, shape, dim)


def turned(value, shift, axis):
    return pltpu.roll(value, shift % value.shape[axis], axis)


def after_y(value):
    return turned(value, -1, 0)


def before_y(value):
    return turned(value, 1, 0)


def after_z(value, ghost):
    return jnp.where(iota(value.shape, 1) == DEPTH - 1, ghost, turned(value, -1, 1))


def before_z(value, ghost):
    return jnp.where(iota(value.shape, 1) == 0, ghost, turned(value, 1, 1))


def coordinates():
    gx = lax.axis_index("gx")
    gy = lax.axis_index("gy")
    return gx, gy // 2, gy % 2


def coupling(half, vn_of, water_of):
    group = iota((SOLID, DEPTH), 1) // 8
    group_w = iota((WATER, DEPTH), 1) // 8
    sub = iota((8, DEPTH), 0)
    velocity = jnp.zeros((SOLID, DEPTH), F32)
    bottom = jnp.zeros((WATER, DEPTH), F32)
    for x in range(XS):
        velocity = jnp.where(group == x, vn_of(x), velocity)
        bottom = jnp.where(group_w == x, water_of(x)[:, DEPTH - 1 : DEPTH], bottom)
    low = half == 0
    zero = jnp.zeros((8, DEPTH), F32)
    own0, own1, own2 = bottom[0:8], bottom[8:16], bottom[16:24]
    keep = (sub < 4) != low
    spread = jnp.concatenate(
        [
            jnp.where(low, own0, zero),
            jnp.where(low, own1, zero),
            jnp.where(low, zero, own0),
            jnp.where(low, zero, own1),
            jnp.where(keep, own2, zero),
        ],
        axis=0,
    )
    return spread, velocity


def own_strip(half, plane_of):
    lane = iota((OWN, DEPTH), 1)
    group = lane // 8
    strip = jnp.zeros((OWN, DEPTH), F32)
    for x in range(XS):
        strip = jnp.where(group == x, turned(plane_of(x), 8 * x + 4, 1), strip)
    return jnp.where((lane % 8 < 4) == (half == 0), strip, 0.0)


def send_strip_faces(strips, a_ref, b_ref, rows):
    even = lax.axis_index("gx") % 2 == 0
    group = iota((SOLID, DEPTH), 1) // 8
    head = tail = jnp.zeros((SOLID, DEPTH), F32)
    for c in range(3):
        head = jnp.where(group == c, turned(strips[c], 8 * c, 1), head)
        tail = jnp.where(group == c, turned(strips[c], 8 * c + 8, 1), tail)
    a_ref[rows] = jnp.where(even, tail, head)
    b_ref[rows] = jnp.where(even, head, tail)


def strip_step(now, old, s, b, contact, pb, before, after):
    lane = iota((SOLID, DEPTH), 1)

    def next_x(value, face):
        return jnp.where(lane >= DEPTH - 8, turned(face, DEPTH - 8, 1), turned(value, -8, 1))

    def prev_x(value, face):
        return jnp.where(lane < 8, face, turned(value, 8, 1))

    def next_z(value):
        return turned(value, -1, 1)

    def prev_z(value):
        return turned(value, 1, 1)

    def x_weight(u1, u2):
        return (after_y(u1) - before_y(u1)) + (next_z(u2) - prev_z(u2))

    shifts = []
    for c in range(3):
        u = now[c]
        shifts.append((
            (next_x(u, after[c]), prev_x(u, before[c])),
            (after_y(u), before_y(u)),
            (next_z(u), prev_z(u)),
        ))
    q = [shifts[c][c][0] - shifts[c][c][1] for c in range(3)]
    wx, wy, wz = q[1] + q[2], q[0] + q[2], q[0] + q[1]
    mixed = [
        next_x(wx, x_weight(after[1], after[2])) - prev_x(wx, x_weight(before[1], before[2])),
        after_y(wy) - before_y(wy),
        next_z(wz) - prev_z(wz),
    ]
    new = []
    for c in range(3):
        u = now[c]
        two = u + u
        sums = [up + down for up, down in shifts[c]]
        laplace = (sums[0] + sums[1] + sums[2]) - 6.0 * u
        grad = (sums[c] - two) + 0.25 * mixed[c]
        value = (two - old[c]) + s * laplace + b * grad
        if c == 2:
            value = value - jnp.where(contact, LOAD * pb, 0.0)
        new.append(value)
    return new


def velocity_of(now, before, contact_field):
    return jnp.sum(
        jnp.where(contact_field == 1.0, now - before, 0.0), axis=1, keepdims=True
    )


def paired(first, second, swap):
    return jnp.where(swap, first, turned(second, 4, 0))


def pack_kernel(
    d_ref, un_hbm, up_hbm, elastic, pressures,
    un, up, s_v, b_v, ya_ref, yb_ref, wo_ref, partner_ref, sems,
):
    gx, block, half = coordinates()
    even = block % 2 == 0
    upper = half == 0
    copies = []
    for k, (src, dst) in enumerate(
        ((un_hbm, un), (up_hbm, up))
    ):
        copy = pltpu.make_async_copy(src, dst, sems.at[k])
        copy.start()
        copies.append(copy)
    pn, pp, c_v = (pressures.at[k] for k in range(3))
    sub = iota((8, DEPTH), 0)
    low = sub < 4
    for inner in (True, False):
        keep = low == (upper != inner)

        def pick(ref, at):
            return jnp.where(upper == inner, ref[at, pl.ds(8, 8)], ref[at, pl.ds(0, 8)])

        tiles = [paired(pick(pn, x), pick(pp, x), keep) for x in range(XS)]
        tiles += [paired(pick(c_v, x), pick(c_v, x + 8), keep) for x in range(8)]
        for at, tile in enumerate(tiles):
            if inner:
                partner_ref[pl.ds(8 * at, 8)] = tile
            else:
                wo_ref[at] = tile
    for x in range(XS):
        inside = d_ref[x] >= 1.0
        s_v[x] = jnp.where(inside, elastic[0, x], 0.0)
        b_v[x] = jnp.where(inside, elastic[1, x], 0.0)
    for k, plane_of in enumerate((lambda x: s_v[x], lambda x: b_v[x], lambda x: d_ref[x])):
        partner_ref[pl.ds(INNER + OWN * (6 + k), OWN)] = own_strip(half, plane_of)
    for copy in copies:
        copy.wait()
    for x in range(XS):
        inside = d_ref[x] >= 1.0
        for ref in (un, up):
            for c in range(3):
                ref[c, x] = jnp.where(inside, ref[c, x], 0.0)
        sides = []
        for side, rows in ((0, pl.ds(0, 8)), (1, pl.ds(24, 8))):
            d = d_ref[x, rows]
            u = [un[c, x, rows] for c in range(3)]
            v = [up[c, x, rows] for c in range(3)]
            spare = 3 if side == 0 else 4
            for c in range(3):
                row = c if side == 0 else 5 + c
                v[c] = jnp.where(sub == spare, turned(d, spare - row, 0), v[c])
            keep = low if side == 0 else jnp.logical_not(low)
            sides.append(
                [paired(u[0], u[1], keep), paired(u[2], v[0], keep),
                 paired(v[1], v[2], keep), paired(s_v[x, rows], b_v[x, rows], keep)]
            )
        for k in range(4):
            head, tail = sides[0][k], sides[1][k]
            ya_ref[k, x] = jnp.where(even, tail, head)
            yb_ref[k, x] = jnp.where(even, head, tail)
    planes = [lambda x, c=c: un[c, x] for c in range(3)]
    planes += [lambda x, c=c: up[c, x] for c in range(3)]
    for k, plane_of in enumerate(planes):
        partner_ref[pl.ds(INNER + OWN * k, OWN)] = own_strip(half, plane_of)


def strip_kernel(own_ref, got_ref, full_ref, ya_ref, yb_ref):
    gx, block, half = coordinates()
    even = block % 2 == 0
    low = iota((8, DEPTH), 0) < 4
    full_ref[...] = own_ref[pl.ds(INNER, 9 * OWN)] + got_ref[pl.ds(INNER, 9 * OWN)]
    for pair in range(5):
        first, second = 2 * pair, min(2 * pair + 1, 8)
        sides = []
        for row, keep in ((0, low), (OWN - 8, jnp.logical_not(low))):
            sides.append(
                paired(full_ref[pl.ds(OWN * first + row, 8)], full_ref[pl.ds(OWN * second + row, 8)], keep)
            )
        ya_ref[pl.ds(8 * pair, 8)] = jnp.where(even, sides[1], sides[0])
        yb_ref[pl.ds(8 * pair, 8)] = jnp.where(even, sides[0], sides[1])


def send_faces(solid_of, water_of, a_ref, b_ref):
    even = lax.axis_index("gx") % 2 == 0
    for c in range(3):
        head, tail = solid_of(c, 0), solid_of(c, XS - 1)
        a_ref[pl.ds(SOLID * c, SOLID)] = jnp.where(even, tail, head)
        b_ref[pl.ds(SOLID * c, SOLID)] = jnp.where(even, head, tail)
    head, tail = water_of(0), water_of(XS - 1)
    a_ref[pl.ds(3 * SOLID, WATER)] = jnp.where(even, tail, head)
    b_ref[pl.ds(3 * SOLID, WATER)] = jnp.where(even, head, tail)


def received(a_ref, b_ref, rows):
    gx = lax.axis_index("gx")
    even = gx % 2 == 0
    a, b = a_ref[rows], b_ref[rows]
    before = jnp.where(gx > 0, jnp.where(even, b, a), 0.0)
    after = jnp.where(gx < lax.axis_size("gx") - 1, jnp.where(even, a, b), 0.0)
    return before, after


def assemble_kernel(
    d_ref, un_ref, up_ref, s_ref, b_ref, pressures,
    ya_ref, yb_ref, wo_ref, partner_ref, full_ref, ysa_ref, ysb_ref,
    u_out, v_out, s_out, b_out, d_out, p_out, q_out, c_out, now_out, old_out, static_out, coupling_out, xa_out, xb_out,
):
    gx, block, half = coordinates()
    even = block % 2 == 0
    sub = iota((8, DEPTH), 0)
    low = sub < 4
    has_before = block > 0
    has_after = block < lax.axis_size("gy") // 2 - 1
    outer = jnp.where(half == 0, has_before, has_after)
    own, beyond = pl.ds(0, OWN), pl.ds(OWN, 8)

    def halos(got_a, got_b):
        from_before = jnp.where(has_before, jnp.where(even, got_b, got_a), 0.0)
        from_after = jnp.where(has_after, jnp.where(even, got_a, got_b), 0.0)
        return (
            jnp.where(low, from_after, from_before),
            turned(jnp.where(low, from_before, from_after), 4, 0),
        )

    strip_halos = []
    for pair in range(5):
        rows = pl.ds(8 * pair, 8)
        strip_halos.extend(halos(ysa_ref[rows], ysb_ref[rows]))
    for k in range(9):
        ref = (now_out, old_out, static_out)[k // 3]
        ref[pl.ds(SOLID * (k % 3), OWN)] = full_ref[pl.ds(OWN * k, OWN)]
        ref[pl.ds(SOLID * (k % 3) + OWN, 8)] = strip_halos[k]
    for x in range(XS):
        for c in range(3):
            u_out[c, x, own] = un_ref[c, x]
            v_out[c, x, own] = up_ref[c, x]
        s_out[x, own] = s_ref[x]
        b_out[x, own] = b_ref[x]
        d_out[x, own] = d_ref[x]
        halo = []
        for k in range(4):
            halo.extend(halos(ya_ref[k, x], yb_ref[k, x]))
        contact_rows = jnp.zeros((8, DEPTH), F32)
        for c in range(3):
            v = halo[3 + c]
            contact_rows = jnp.where(sub == c, turned(v, c - 3, 0), contact_rows)
            contact_rows = jnp.where(sub == 5 + c, turned(v, 1 + c, 0), contact_rows)
        halo.append(contact_rows)
        for c in range(3):
            u_out[c, x, beyond] = halo[c]
            v_out[c, x, beyond] = halo[3 + c]
        s_out[x, beyond] = halo[6]
        b_out[x, beyond] = halo[7]
        d_out[x, beyond] = halo[8]
        pn_ref, pp_ref, c_ref = (pressures.at[k] for k in range(3))
        from_partner = low == (half == 0)

        def water_halo(at, natural):
            inner, beyond_it = partner_ref[pl.ds(8 * at, 8)], jnp.where(outer, wo_ref[at], 0.0)
            if not natural:
                inner, beyond_it = turned(inner, 4, 0), turned(beyond_it, 4, 0)
            return jnp.where(from_partner, inner, beyond_it)

        for ref, out, at, natural in (
            (pn_ref, p_out, x, True), (pp_ref, q_out, x, False), (c_ref, c_out, XS + x % 8, x < 8)
        ):
            out[x, pl.ds(0, 16)] = ref[x]
            out[x, pl.ds(16, 8)] = water_halo(at, natural)
    bottom, velocity = coupling(
        half,
        lambda x: velocity_of(u_out[2, x], v_out[2, x], d_out[x]),
        lambda x: p_out[x],
    )
    coupling_out[pl.ds(0, SOLID)] = bottom
    coupling_out[pl.ds(SOLID, SOLID)] = velocity
    strips = [now_out[pl.ds(SOLID * c, SOLID)] for c in range(3)]
    send_strip_faces(strips, xa_out, xb_out, pl.ds(FACE, SOLID))
    send_faces(lambda c, x: u_out[c, x], lambda x: p_out[x], xa_out, xb_out)


def step_kernel(last, lags, *refs):
    u_ref, v_ref, s_ref, b_ref, d_ref, p_ref, q_ref, c_ref = refs[0:8]
    now_ref, old_ref, static_ref, own_ref, got_ref, xa_ref, xb_ref = refs[8:15]
    strip_rows = pl.ds(FACE, SOLID)
    u_out, p_out = refs[15:17]
    more = refs[17:]
    gx, block, half = coordinates()
    low_half = half == 0
    shape = (SOLID, DEPTH)
    lane = iota(shape, 1)
    at_edge = lane == jnp.where(low_half, DEPTH - 1, 0)
    sub = iota((8, DEPTH), 0)
    bottom = own_ref[pl.ds(0, SOLID)] + got_ref[pl.ds(0, SOLID)]
    velocity = own_ref[pl.ds(SOLID, SOLID)] + got_ref[pl.ds(SOLID, SOLID)]
    strips = [now_ref[pl.ds(SOLID * c, SOLID)] for c in range(3)]
    strip_before, strip_after = [], []
    for value, out in zip(received(xa_ref, xb_ref, strip_rows), (strip_before, strip_after)):
        out.extend(turned(value, -8 * c, 1) if c else value for c in range(3))

    def of_half(value):
        return jnp.where(low_half, value, turned(value, 2, 1))

    ghosts = [[of_half(v) for v in group] for group in (strip_before, strips, strip_after)]

    def ghost(c, x):
        if x < 0:
            source, shift = ghosts[0][c], 123
        elif x >= XS:
            source, shift = ghosts[2][c], 123
        else:
            source, shift = ghosts[1][c], 123 - 8 * x
        return jnp.where(at_edge, turned(source, shift, 1), 0.0)

    faces = [received(xa_ref, xb_ref, pl.ds(SOLID * c, SOLID)) for c in range(3)]
    faces.append(received(xa_ref, xb_ref, pl.ds(3 * SOLID, WATER)))

    def solid(c, x):
        if x < 0:
            return faces[c][0]
        if x >= XS:
            return faces[c][1]
        return u_ref[c, x]

    def water(x):
        if x < 0:
            return faces[3][0]
        if x >= XS:
            return faces[3][1]
        return p_ref[x]

    def plane(x):
        uy, uz = solid(1, x), solid(2, x)
        gz = ghost(2, x)
        up, down = after_y(uy), before_y(uy)
        deep, shallow = after_z(uz, gz), before_z(uz, gz)
        return up - down, up + down, deep - shallow, deep + shallow

    behind = plane(-1)
    here = plane(0)
    ghost_x_behind, ghost_x_here = ghost(0, -1), ghost(0, 0)
    for x in range(XS):
        ahead = plane(x + 1)
        ghost_x_ahead = ghost(0, x + 1)
        qy, sy_y, qz, sz_z = here
        now = [solid(c, x) for c in range(3)]
        nxt = [solid(c, x + 1) for c in range(3)]
        prv = [solid(c, x - 1) for c in range(3)]
        qx = nxt[0] - prv[0]
        sum_x = [nxt[c] + prv[c] for c in range(3)]
        dx = (ahead[0] + ahead[2]) - (behind[0] + behind[2])
        wy = qx + qz
        dy = after_y(wy) - before_y(wy)
        gy_here = ghost(1, x)
        wz = qx + qy
        ghost_wz = (ghost_x_ahead - ghost_x_behind) + (after_y(gy_here) - before_y(gy_here))
        dz = after_z(wz, ghost_wz) - before_z(wz, ghost_wz)
        sum_y = [after_y(now[0]) + before_y(now[0]), sy_y, after_y(now[2]) + before_y(now[2])]
        sum_z = [
            after_z(now[0], ghost_x_here) + before_z(now[0], ghost_x_here),
            after_z(now[1], gy_here) + before_z(now[1], gy_here),
            sz_z,
        ]
        own_sums = [sum_x[0], sum_y[1], sum_z[2]]
        mixed = [dx, dy, dz]
        s, b = s_ref[x], b_ref[x]
        d = d_ref[x]
        contact = d == 1.0
        pb = jnp.broadcast_to(bottom[:, 8 * x : 8 * x + 1], shape)
        vn = jnp.broadcast_to(velocity[:, 8 * x : 8 * x + 1], shape)
        for c in range(3):
            u = now[c]
            two = u + u
            laplace = (sum_x[c] + sum_y[c] + sum_z[c]) - 6.0 * u
            grad = (own_sums[c] - two) + 0.25 * mixed[c]
            new = (two - v_ref[c, x]) + s * laplace + b * grad
            if c == 2:
                new = new - jnp.where(contact, LOAD * pb, 0.0)
            if last:
                u_out[c, x] = new[0:32]
            else:
                u_out[c, x] = new
        beyond = jnp.where(
            sub < 4,
            jnp.where(low_half, vn[16:24], vn[32:40]),
            jnp.where(low_half, vn[32:40], vn[8:16]),
        )
        vn_water = jnp.concatenate([jnp.where(low_half, vn[0:16], vn[16:32]), beyond], axis=0)
        p = water(x)
        lateral = water(x + 1) + water(x - 1) + after_y(p) + before_y(p)
        vertical = after_z(p, p - vn_water) + before_z(p, 0.0)
        p_new = (2.0 * p - q_ref[x]) + c_ref[x] * (lateral + vertical - 6.0 * p)
        if last:
            p_out[x] = p_new[0:16]
        else:
            p_out[x] = p_new
        behind, here = here, ahead
        ghost_x_behind, ghost_x_here = ghost_x_here, ghost_x_ahead
    if lags:
        lag_a, lag_b = more[-2:]
        even = gx % 2 == 0
        for n, ref in enumerate((u_ref, u_out)[2 - lags :]):
            for k in range(LAG):
                head = ref[2, k, pl.ds(0, 32)]
                tail = ref[2, k + XS - LAG, pl.ds(0, 32)]
                lag_a[n, k] = jnp.where(even, tail, head)
                lag_b[n, k] = jnp.where(even, head, tail)
    if last:
        for x in range(XS):
            more[0][x] = u_out[2, x]
        return
    strip_out, coupling_out, xa_out, xb_out = more[:4]
    static = [static_ref[pl.ds(SOLID * k, SOLID)] for k in range(3)]
    old = [old_ref[pl.ds(SOLID * c, SOLID)] for c in range(3)]
    strips = strip_step(
        strips, old, static[0], static[1], static[2] == 1.0, bottom, strip_before, strip_after
    )
    for c in range(3):
        strip_out[pl.ds(SOLID * c, SOLID)] = strips[c]
    send_strip_faces(strips, xa_out, xb_out, pl.ds(FACE, SOLID))
    send_faces(lambda c, x: u_out[c, x], lambda x: p_out[x], xa_out, xb_out)
    bottom, velocity = coupling(
        half,
        lambda x: velocity_of(u_out[2, x], u_ref[2, x], d_ref[x]),
        lambda x: p_out[x],
    )
    coupling_out[pl.ds(0, SOLID)] = bottom
    coupling_out[pl.ds(SOLID, SOLID)] = velocity


def own_range(lag):
    return max(0, LAG - lag), min(XS, XS + LAG - lag)


def open_pairs():
    pairs = []
    for lag in range(2 * LAG + 1):
        low, high = own_range(lag)
        pairs.extend((lag, x) for x in range(XS) if not low <= x < high)
    return {pair: at for at, pair in enumerate(pairs)}


def lag_halos(a, b):
    gx = lax.axis_index("gx")
    even = gx % 2 == 0
    before = jnp.where(gx > 0, jnp.where(even, b, a), 0.0)
    after = jnp.where(gx < lax.axis_size("gx") - 1, jnp.where(even, a, b), 0.0)
    return before, after


def image_kernel(
    u0, u1, u2, u3, a_ref, b_ref, recv_ref,
    out_hbm, open_ref, halo, weights, stage, sems,
):
    for t in range(2):
        for k in range(LAG):
            halo[t, k], halo[t, LAG + k] = lag_halos(a_ref[t, k], b_ref[t, k])
    for t in range(STEPS):
        for x in range(XS):
            weights[t, x] = recv_ref[t, x].astype(F32)

    def column(t, x):
        if x < 0:
            return halo[t, x + LAG]
        if x >= XS:
            return halo[t, x - XS + LAG]
        if t == STEPS - 1:
            return u3[x]
        return (u0, u1, u2)[t][2, x, pl.ds(0, OWN)]

    pairs = open_pairs()
    copies = []
    for lag in range(2 * LAG + 1):
        low, high = own_range(lag)
        for x in range(XS):
            at = x + lag - LAG
            total = column(0, at) * weights[0, x]
            total = total + column(1, at) * weights[1, x]
            if low <= x < high:
                total = total + column(2, at) * weights[2, x]
                total = total + column(3, at) * weights[3, x]
                stage[lag, x] = total.astype(jnp.bfloat16)
            else:
                open_ref[pairs[lag, x]] = total
        columns = pl.ds(low, high - low)
        copy = pltpu.make_async_copy(
            stage.at[lag, columns], out_hbm.at[lag, columns], sems.at[lag]
        )
        copy.start()
        copies.append(copy)
    for copy in copies:
        copy.wait()


def finish_kernel(open_ref, a_ref, b_ref, recv_ref, image_hbm, out_hbm, halo, stage, sems):
    for t in range(2):
        for k in range(LAG):
            halo[t, k], halo[t, LAG + k] = lag_halos(a_ref[t, k], b_ref[t, k])
    pairs = open_pairs()
    copies = []
    for n, lag in enumerate(k for k in range(2 * LAG + 1) if k != LAG):
        low, high = own_range(lag)
        start, stop = (0, low) if lag < LAG else (high, XS)
        for x in range(start, stop):
            at = x + lag if lag < LAG else x + lag - XS
            total = open_ref[pairs[lag, x]] + halo[0, at] * recv_ref[2, x].astype(F32)
            total = total + halo[1, at] * recv_ref[3, x].astype(F32)
            stage[lag, x] = total.astype(jnp.bfloat16)
        columns = pl.ds(start, stop - start)
        copy = pltpu.make_async_copy(
            stage.at[lag, columns], out_hbm.at[lag, columns], sems.at[n]
        )
        copy.start()
        copies.append(copy)
    for copy in copies:
        copy.wait()


def call(body, outs, *args, specs=None, scratch=(), limit=40):
    return pl.pallas_call(
        body,
        out_shape=[jax.ShapeDtypeStruct(shape, F32) for shape in outs],
        in_specs=specs or [VMEM] * len(args),
        out_specs=[VMEM] * len(outs),
        scratch_shapes=list(scratch),
        compiler_params=pltpu.CompilerParams(vmem_limit_bytes=int(limit * 1024 * 1024)),
    )(*args)


def swapped(size, width):
    return [(i, i ^ width) for i in range(size)]


def crossed(size, width):
    return [(i, (((i + width) % size ^ width) - width) % size) for i in range(size)]


def on_device(p_now, p_prev, water_coef, seafloor, u_now, u_prev, shear, bulk, recv_field):
    size_x = lax.axis_size("gx")
    size_y = lax.axis_size("gy")
    half = lax.axis_index("gy") % 2
    far = jnp.where(half == 0, 4 * DEPTH, -4 * DEPTH)
    levels = jnp.where(seafloor >= 0, seafloor, far)[:, :, None]
    depth = jnp.arange(1, DEPTH + 1, dtype=jnp.int32)[None, None, :]
    field = (depth - levels).astype(F32)
    pressures = jnp.stack([p_now, p_prev, water_coef])
    raw = (field, u_now, u_prev, jnp.stack([shear, bulk]), pressures)
    tile = (XS, 8, DEPTH)
    y_payload = (4,) + tile
    w_payload = (XS + XS // 2, 8, DEPTH)
    hbm = pl.BlockSpec(memory_space=pltpu.HBM)
    *masked, ya, yb, w_out, to_partner = call(
        pack_kernel,
        [u_now.shape, u_now.shape, shear.shape, shear.shape, y_payload, y_payload, w_payload, (INNER + 9 * OWN, DEPTH)],
        *raw,
        specs=[VMEM, hbm, hbm, VMEM, VMEM],
        scratch=[pltpu.SemaphoreType.DMA((2,))],
        limit=PACK_LIMIT,
    )

    def to_y(first, second):
        return (
            lax.ppermute(first, "gy", swapped(size_y, 2)),
            lax.ppermute(second, "gy", crossed(size_y, 2)),
        )

    partner = lax.ppermute(to_partner, "gy", swapped(size_y, 1))
    ya, yb = to_y(ya, yb)
    w_out = lax.ppermute(w_out, "gy", crossed(size_y, 1))
    y_strip = (SOLID, DEPTH)
    full, ysa, ysb = call(strip_kernel, [(9 * OWN, DEPTH), y_strip, y_strip], to_partner, partner)
    ysa, ysb = to_y(ysa, ysb)
    solid = (XS, SOLID, DEPTH)
    water = (XS, WATER, DEPTH)
    face = (FACE + SOLID, DEPTH)
    strip = (3 * SOLID, DEPTH)
    pair = (2 * SOLID, DEPTH)
    u, v, s, b, d, p, q, c, now, old, static, own, xa, xb = call(
        assemble_kernel,
        [(3,) + solid, (3,) + solid, solid, solid, solid, water, water, water,
         strip, strip, strip, pair, face, face],
        field, *masked, pressures, ya, yb, w_out, partner, full, ysa, ysb,
    )

    def to_x(first, second):
        return (
            lax.ppermute(first, "gx", swapped(size_x, 1)),
            lax.ppermute(second, "gx", crossed(size_x, 1)),
        )

    got = lax.ppermute(own, "gy", swapped(size_y, 1))
    faces = to_x(xa, xb)
    verticals, reaches = [], []
    for t in range(STEPS):
        last = t == STEPS - 1
        lags = (0, 2, 0, 2)[t]
        if last:
            outs = [(3, XS, 32, DEPTH), (XS, 16, DEPTH), (XS, 32, DEPTH)]
        else:
            outs = [(3,) + solid, water, strip, pair, face, face]
        outs = outs + [(lags, LAG, 32, DEPTH)] * (2 if lags else 0)

        def body(*refs, last=last, lags=lags):
            step_kernel(last, lags, *refs)

        u_new, p_new, *more = call(
            body, outs, u, v, s, b, d, p, q, c, now, old, static, own, got, *faces
        )
        v, u, q, p = u, u_new, p, p_new
        if last:
            verticals.append(more[0])
        else:
            verticals.append(u)
            old, now, own = now, more[0], more[1]
            faces = to_x(more[2], more[3])
            got = lax.ppermute(own, "gy", swapped(size_y, 1))
        if lags:
            reaches += to_x(more[-2], more[-1])
    lags = 2 * LAG + 1
    image_shape = jax.ShapeDtypeStruct((lags, XS, OWN, DEPTH), jnp.bfloat16)
    open_shape = jax.ShapeDtypeStruct((len(open_pairs()), OWN, DEPTH), F32)
    stage = pltpu.VMEM(image_shape.shape, jnp.bfloat16)
    image, unfinished = pl.pallas_call(
        image_kernel,
        out_shape=[image_shape, open_shape],
        in_specs=[VMEM] * 7,
        out_specs=[hbm, VMEM],
        scratch_shapes=[
            pltpu.VMEM((2, 2 * LAG, OWN, DEPTH), F32),
            pltpu.VMEM((STEPS, XS, OWN, DEPTH), F32),
            stage,
            pltpu.SemaphoreType.DMA((lags,)),
        ],
        compiler_params=PARAMS,
    )(*verticals, *reaches[0:2], recv_field)
    image = pl.pallas_call(
        finish_kernel,
        out_shape=image_shape,
        in_specs=[VMEM] * 4 + [hbm],
        out_specs=hbm,
        scratch_shapes=[
            pltpu.VMEM((2, 2 * LAG, OWN, DEPTH), F32),
            stage,
            pltpu.SemaphoreType.DMA((lags - 1,)),
        ],
        input_output_aliases={4: 0},
        compiler_params=PARAMS,
    )(unfinished, *reaches[2:4], recv_field, image)
    return (p, u, image)


def solution(mesh):
    return jax.shard_map(
        on_device,
        mesh=mesh,
        in_specs=(
            P("gx", "gy", None),
            P("gx", "gy", None),
            P("gx", "gy", None),
            P("gx", "gy"),
            P(None, "gx", "gy", None),
            P(None, "gx", "gy", None),
            P("gx", "gy", None),
            P("gx", "gy", None),
            P(None, "gx", "gy", None),
        ),
        out_specs=(P("gx", "gy", None), P(None, "gx", "gy", None), P(None, "gx", "gy", None)),
        check_vma=False,
    )
```

```python
import jax
import jax.numpy as jnp
from jax import lax
from jax.experimental import pallas as pl
from jax.experimental.pallas import tpu as pltpu
from jax.sharding import PartitionSpec as P

LAG = 10
STEPS = 4
LOAD = 0.5
F32 = jnp.float32
XS = 16
SOLID = 40
WATER = 24
DEPTH = 128
FACE = 3 * SOLID + WATER
OWN = 32
INNER = 192
VMEM = pl.BlockSpec(memory_space=pltpu.VMEM)
PACK_LIMIT = 49.5
PARAMS = pltpu.CompilerParams(vmem_limit_bytes=40 * 1024 * 1024)


def iota(shape, dim):
    return lax.broadcasted_iota(jnp.int32, shape, dim)


def turned(value, shift, axis):
    return pltpu.roll(value, shift % value.shape[axis], axis)


def after_y(value):
    return turned(value, -1, 0)


def before_y(value):
    return turned(value, 1, 0)


def after_z(value, ghost):
    return jnp.where(iota(value.shape, 1) == DEPTH - 1, ghost, turned(value, -1, 1))


def before_z(value, ghost):
    return jnp.where(iota(value.shape, 1) == 0, ghost, turned(value, 1, 1))


def coordinates():
    gx = lax.axis_index("gx")
    gy = lax.axis_index("gy")
    return gx, gy // 2, gy % 2


def coupling(half, vn_of, water_of):
    group = iota((SOLID, DEPTH), 1) // 8
    group_w = iota((WATER, DEPTH), 1) // 8
    sub = iota((8, DEPTH), 0)
    velocity = jnp.zeros((SOLID, DEPTH), F32)
    bottom = jnp.zeros((WATER, DEPTH), F32)
    for x in range(XS):
        velocity = jnp.where(group == x, vn_of(x), velocity)
        bottom = jnp.where(group_w == x, water_of(x)[:, DEPTH - 1 : DEPTH], bottom)
    low = half == 0
    zero = jnp.zeros((8, DEPTH), F32)
    own0, own1, own2 = bottom[0:8], bottom[8:16], bottom[16:24]
    keep = (sub < 4) != low
    spread = jnp.concatenate(
        [
            jnp.where(low, own0, zero),
            jnp.where(low, own1, zero),
            jnp.where(low, zero, own0),
            jnp.where(low, zero, own1),
            jnp.where(keep, own2, zero),
        ],
        axis=0,
    )
    return spread, velocity


def own_strip(half, plane_of):
    lane = iota((OWN, DEPTH), 1)
    group = lane // 8
    strip = jnp.zeros((OWN, DEPTH), F32)
    for x in range(XS):
        strip = jnp.where(group == x, turned(plane_of(x), 8 * x + 4, 1), strip)
    return jnp.where((lane % 8 < 4) == (half == 0), strip, 0.0)


def send_strip_faces(strips, a_ref, b_ref, rows):
    even = lax.axis_index("gx") % 2 == 0
    group = iota((SOLID, DEPTH), 1) // 8
    head = tail = jnp.zeros((SOLID, DEPTH), F32)
    for c in range(3):
        head = jnp.where(group == c, turned(strips[c], 8 * c, 1), head)
        tail = jnp.where(group == c, turned(strips[c], 8 * c + 8, 1), tail)
    a_ref[rows] = jnp.where(even, tail, head)
    b_ref[rows] = jnp.where(even, head, tail)


def strip_step(now, old, s, b, contact, pb, before, after):
    lane = iota((SOLID, DEPTH), 1)

    def next_x(value, face):
        return jnp.where(lane >= DEPTH - 8, turned(face, DEPTH - 8, 1), turned(value, -8, 1))

    def prev_x(value, face):
        return jnp.where(lane < 8, face, turned(value, 8, 1))

    def next_z(value):
        return turned(value, -1, 1)

    def prev_z(value):
        return turned(value, 1, 1)

    def x_weight(u1, u2):
        return (after_y(u1) - before_y(u1)) + (next_z(u2) - prev_z(u2))

    shifts = []
    for c in range(3):
        u = now[c]
        shifts.append((
            (next_x(u, after[c]), prev_x(u, before[c])),
            (after_y(u), before_y(u)),
            (next_z(u), prev_z(u)),
        ))
    q = [shifts[c][c][0] - shifts[c][c][1] for c in range(3)]
    wx, wy, wz = q[1] + q[2], q[0] + q[2], q[0] + q[1]
    mixed = [
        next_x(wx, x_weight(after[1], after[2])) - prev_x(wx, x_weight(before[1], before[2])),
        after_y(wy) - before_y(wy),
        next_z(wz) - prev_z(wz),
    ]
    new = []
    for c in range(3):
        u = now[c]
        two = u + u
        sums = [up + down for up, down in shifts[c]]
        laplace = (sums[0] + sums[1] + sums[2]) - 6.0 * u
        grad = (sums[c] - two) + 0.25 * mixed[c]
        value = (two - old[c]) + s * laplace + b * grad
        if c == 2:
            value = value - jnp.where(contact, LOAD * pb, 0.0)
        new.append(value)
    return new


def velocity_of(now, before, contact_field):
    return jnp.sum(
        jnp.where(contact_field == 1.0, now - before, 0.0), axis=1, keepdims=True
    )


def paired(first, second, swap):
    return jnp.where(swap, first, turned(second, 4, 0))


def pack_kernel(
    d_ref, un_hbm, up_hbm, elastic, pressures,
    un, up, s_v, b_v, ya_ref, yb_ref, wo_ref, partner_ref, sems,
):
    gx, block, half = coordinates()
    even = block % 2 == 0
    upper = half == 0
    copies = []
    for k, (src, dst) in enumerate(
        ((un_hbm, un), (up_hbm, up))
    ):
        copy = pltpu.make_async_copy(src, dst, sems.at[k])
        copy.start()
        copies.append(copy)
    pn, pp, c_v = (pressures.at[k] for k in range(3))
    sub = iota((8, DEPTH), 0)
    low = sub < 4
    for inner in (True, False):
        keep = low == (upper != inner)

        def pick(ref, at):
            return jnp.where(upper == inner, ref[at, pl.ds(8, 8)], ref[at, pl.ds(0, 8)])

        tiles = [paired(pick(pn, x), pick(pp, x), keep) for x in range(XS)]
        tiles += [paired(pick(c_v, x), pick(c_v, x + 8), keep) for x in range(8)]
        for at, tile in enumerate(tiles):
            if inner:
                partner_ref[pl.ds(8 * at, 8)] = tile
            else:
                wo_ref[at] = tile
    for x in range(XS):
        inside = d_ref[x] >= 1.0
        s_v[x] = jnp.where(inside, elastic[0, x], 0.0)
        b_v[x] = jnp.where(inside, elastic[1, x], 0.0)
    for k, plane_of in enumerate((lambda x: s_v[x], lambda x: b_v[x], lambda x: d_ref[x])):
        partner_ref[pl.ds(INNER + OWN * (6 + k), OWN)] = own_strip(half, plane_of)
    for copy in copies:
        copy.wait()
    for x in range(XS):
        inside = d_ref[x] >= 1.0
        for ref in (un, up):
            for c in range(3):
                ref[c, x] = jnp.where(inside, ref[c, x], 0.0)
        sides = []
        for side, rows in ((0, pl.ds(0, 8)), (1, pl.ds(24, 8))):
            d = d_ref[x, rows]
            u = [un[c, x, rows] for c in range(3)]
            v = [up[c, x, rows] for c in range(3)]
            spare = 3 if side == 0 else 4
            for c in range(3):
                row = c if side == 0 else 5 + c
                v[c] = jnp.where(sub == spare, turned(d, spare - row, 0), v[c])
            keep = low if side == 0 else jnp.logical_not(low)
            sides.append(
                [paired(u[0], u[1], keep), paired(u[2], v[0], keep),
                 paired(v[1], v[2], keep), paired(s_v[x, rows], b_v[x, rows], keep)]
            )
        for k in range(4):
            head, tail = sides[0][k], sides[1][k]
            ya_ref[k, x] = jnp.where(even, tail, head)
            yb_ref[k, x] = jnp.where(even, head, tail)
    planes = [lambda x, c=c: un[c, x] for c in range(3)]
    planes += [lambda x, c=c: up[c, x] for c in range(3)]
    for k, plane_of in enumerate(planes):
        partner_ref[pl.ds(INNER + OWN * k, OWN)] = own_strip(half, plane_of)


def strip_kernel(own_ref, got_ref, full_ref, ya_ref, yb_ref):
    gx, block, half = coordinates()
    even = block % 2 == 0
    low = iota((8, DEPTH), 0) < 4
    full_ref[...] = own_ref[pl.ds(INNER, 9 * OWN)] + got_ref[pl.ds(INNER, 9 * OWN)]
    for pair in range(5):
        first, second = 2 * pair, min(2 * pair + 1, 8)
        sides = []
        for row, keep in ((0, low), (OWN - 8, jnp.logical_not(low))):
            sides.append(
                paired(full_ref[pl.ds(OWN * first + row, 8)], full_ref[pl.ds(OWN * second + row, 8)], keep)
            )
        ya_ref[pl.ds(8 * pair, 8)] = jnp.where(even, sides[1], sides[0])
        yb_ref[pl.ds(8 * pair, 8)] = jnp.where(even, sides[0], sides[1])


def send_faces(solid_of, water_of, a_ref, b_ref):
    even = lax.axis_index("gx") % 2 == 0
    for c in range(3):
        head, tail = solid_of(c, 0), solid_of(c, XS - 1)
        a_ref[pl.ds(SOLID * c, SOLID)] = jnp.where(even, tail, head)
        b_ref[pl.ds(SOLID * c, SOLID)] = jnp.where(even, head, tail)
    head, tail = water_of(0), water_of(XS - 1)
    a_ref[pl.ds(3 * SOLID, WATER)] = jnp.where(even, tail, head)
    b_ref[pl.ds(3 * SOLID, WATER)] = jnp.where(even, head, tail)


def received(a_ref, b_ref, rows):
    gx = lax.axis_index("gx")
    even = gx % 2 == 0
    a, b = a_ref[rows], b_ref[rows]
    before = jnp.where(gx > 0, jnp.where(even, b, a), 0.0)
    after = jnp.where(gx < lax.axis_size("gx") - 1, jnp.where(even, a, b), 0.0)
    return before, after


def assemble_kernel(
    d_ref, un_ref, up_ref, s_ref, b_ref, pressures,
    ya_ref, yb_ref, wo_ref, partner_ref, full_ref, ysa_ref, ysb_ref,
    u_out, v_out, s_out, b_out, d_out, p_out, q_out, c_out, now_out, old_out, static_out, coupling_out, xa_out, xb_out,
):
    gx, block, half = coordinates()
    even = block % 2 == 0
    sub = iota((8, DEPTH), 0)
    low = sub < 4
    has_before = block > 0
    has_after = block < lax.axis_size("gy") // 2 - 1
    outer = jnp.where(half == 0, has_before, has_after)
    own, beyond = pl.ds(0, OWN), pl.ds(OWN, 8)

    def halos(got_a, got_b):
        from_before = jnp.where(has_before, jnp.where(even, got_b, got_a), 0.0)
        from_after = jnp.where(has_after, jnp.where(even, got_a, got_b), 0.0)
        return (
            jnp.where(low, from_after, from_before),
            turned(jnp.where(low, from_before, from_after), 4, 0),
        )

    strip_halos = []
    for pair in range(5):
        rows = pl.ds(8 * pair, 8)
        strip_halos.extend(halos(ysa_ref[rows], ysb_ref[rows]))
    for k in range(9):
        ref = (now_out, old_out, static_out)[k // 3]
        ref[pl.ds(SOLID * (k % 3), OWN)] = full_ref[pl.ds(OWN * k, OWN)]
        ref[pl.ds(SOLID * (k % 3) + OWN, 8)] = strip_halos[k]
    for x in range(XS):
        for c in range(3):
            u_out[c, x, own] = un_ref[c, x]
            v_out[c, x, own] = up_ref[c, x]
        s_out[x, own] = s_ref[x]
        b_out[x, own] = b_ref[x]
        d_out[x, own] = d_ref[x]
        halo = []
        for k in range(4):
            halo.extend(halos(ya_ref[k, x], yb_ref[k, x]))
        contact_rows = jnp.zeros((8, DEPTH), F32)
        for c in range(3):
            v = halo[3 + c]
            contact_rows = jnp.where(sub == c, turned(v, c - 3, 0), contact_rows)
            contact_rows = jnp.where(sub == 5 + c, turned(v, 1 + c, 0), contact_rows)
        halo.append(contact_rows)
        for c in range(3):
            u_out[c, x, beyond] = halo[c]
            v_out[c, x, beyond] = halo[3 + c]
        s_out[x, beyond] = halo[6]
        b_out[x, beyond] = halo[7]
        d_out[x, beyond] = halo[8]
        pn_ref, pp_ref, c_ref = (pressures.at[k] for k in range(3))
        from_partner = low == (half == 0)

        def water_halo(at, natural):
            inner, beyond_it = partner_ref[pl.ds(8 * at, 8)], jnp.where(outer, wo_ref[at], 0.0)
            if not natural:
                inner, beyond_it = turned(inner, 4, 0), turned(beyond_it, 4, 0)
            return jnp.where(from_partner, inner, beyond_it)

        for ref, out, at, natural in (
            (pn_ref, p_out, x, True), (pp_ref, q_out, x, False), (c_ref, c_out, XS + x % 8, x < 8)
        ):
            out[x, pl.ds(0, 16)] = ref[x]
            out[x, pl.ds(16, 8)] = water_halo(at, natural)
    bottom, velocity = coupling(
        half,
        lambda x: velocity_of(u_out[2, x], v_out[2, x], d_out[x]),
        lambda x: p_out[x],
    )
    coupling_out[pl.ds(0, SOLID)] = bottom
    coupling_out[pl.ds(SOLID, SOLID)] = velocity
    strips = [now_out[pl.ds(SOLID * c, SOLID)] for c in range(3)]
    send_strip_faces(strips, xa_out, xb_out, pl.ds(FACE, SOLID))
    send_faces(lambda c, x: u_out[c, x], lambda x: p_out[x], xa_out, xb_out)


def step_kernel(last, lags, *refs):
    u_ref, v_ref, s_ref, b_ref, d_ref, p_ref, q_ref, c_ref = refs[0:8]
    now_ref, old_ref, static_ref, own_ref, got_ref, xa_ref, xb_ref = refs[8:15]
    strip_rows = pl.ds(FACE, SOLID)
    u_out, p_out = refs[15:17]
    more = refs[17:]
    gx, block, half = coordinates()
    low_half = half == 0
    shape = (SOLID, DEPTH)
    lane = iota(shape, 1)
    facing = lane % 8 == jnp.where(low_half, 4, 5)
    sub = iota((8, DEPTH), 0)
    bottom = own_ref[pl.ds(0, SOLID)] + got_ref[pl.ds(0, SOLID)]
    velocity = own_ref[pl.ds(SOLID, SOLID)] + got_ref[pl.ds(SOLID, SOLID)]
    strips = [now_ref[pl.ds(SOLID * c, SOLID)] for c in range(3)]
    strip_before, strip_after = [], []
    for value, out in zip(received(xa_ref, xb_ref, strip_rows), (strip_before, strip_after)):
        out.extend(turned(value, -8 * c, 1) if c else value for c in range(3))

    def of_half(value):
        return jnp.where(facing, jnp.where(low_half, value, turned(value, 2, 1)), 0.0)

    ghosts = [[of_half(v) for v in group] for group in (strip_before, strips, strip_after)]

    def ghost(c, x):
        if x < 0:
            source, shift = ghosts[0][c], 123
        elif x >= XS:
            source, shift = ghosts[2][c], 123
        else:
            source, shift = ghosts[1][c], 123 - 8 * x
        return turned(source, shift, 1)

    faces = [received(xa_ref, xb_ref, pl.ds(SOLID * c, SOLID)) for c in range(3)]
    faces.append(received(xa_ref, xb_ref, pl.ds(3 * SOLID, WATER)))

    def solid(c, x):
        if x < 0:
            return faces[c][0]
        if x >= XS:
            return faces[c][1]
        return u_ref[c, x]

    def water(x):
        if x < 0:
            return faces[3][0]
        if x >= XS:
            return faces[3][1]
        return p_ref[x]

    def plane(x):
        uy, uz = solid(1, x), solid(2, x)
        gz = ghost(2, x)
        up, down = after_y(uy), before_y(uy)
        deep, shallow = after_z(uz, gz), before_z(uz, gz)
        return up - down, up + down, deep - shallow, deep + shallow

    behind = plane(-1)
    here = plane(0)
    ghost_x_behind, ghost_x_here = ghost(0, -1), ghost(0, 0)
    for x in range(XS):
        ahead = plane(x + 1)
        ghost_x_ahead = ghost(0, x + 1)
        qy, sy_y, qz, sz_z = here
        now = [solid(c, x) for c in range(3)]
        nxt = [solid(c, x + 1) for c in range(3)]
        prv = [solid(c, x - 1) for c in range(3)]
        qx = nxt[0] - prv[0]
        sum_x = [nxt[c] + prv[c] for c in range(3)]
        dx = (ahead[0] + ahead[2]) - (behind[0] + behind[2])
        wy = qx + qz
        dy = after_y(wy) - before_y(wy)
        gy_here = ghost(1, x)
        wz = qx + qy
        ghost_wz = (ghost_x_ahead - ghost_x_behind) + (after_y(gy_here) - before_y(gy_here))
        dz = after_z(wz, ghost_wz) - before_z(wz, ghost_wz)
        sum_y = [after_y(now[0]) + before_y(now[0]), sy_y, after_y(now[2]) + before_y(now[2])]
        sum_z = [
            after_z(now[0], ghost_x_here) + before_z(now[0], ghost_x_here),
            after_z(now[1], gy_here) + before_z(now[1], gy_here),
            sz_z,
        ]
        own_sums = [sum_x[0], sum_y[1], sum_z[2]]
        mixed = [dx, dy, dz]
        s, b = s_ref[x], b_ref[x]
        d = d_ref[x]
        contact = d == 1.0
        pb = jnp.broadcast_to(bottom[:, 8 * x : 8 * x + 1], shape)
        vn = jnp.broadcast_to(velocity[:, 8 * x : 8 * x + 1], shape)
        for c in range(3):
            u = now[c]
            two = u + u
            laplace = (sum_x[c] + sum_y[c] + sum_z[c]) - 6.0 * u
            grad = (own_sums[c] - two) + 0.25 * mixed[c]
            new = (two - v_ref[c, x]) + s * laplace + b * grad
            if c == 2:
                new = new - jnp.where(contact, LOAD * pb, 0.0)
            if last:
                u_out[c, x] = new[0:32]
            else:
                u_out[c, x] = new
        beyond = jnp.where(
            sub < 4,
            jnp.where(low_half, vn[16:24], vn[32:40]),
            jnp.where(low_half, vn[32:40], vn[8:16]),
        )
        vn_water = jnp.concatenate([jnp.where(low_half, vn[0:16], vn[16:32]), beyond], axis=0)
        p = water(x)
        lateral = water(x + 1) + water(x - 1) + after_y(p) + before_y(p)
        vertical = after_z(p, p - vn_water) + before_z(p, 0.0)
        p_new = (2.0 * p - q_ref[x]) + c_ref[x] * (lateral + vertical - 6.0 * p)
        if last:
            p_out[x] = p_new[0:16]
        else:
            p_out[x] = p_new
        behind, here = here, ahead
        ghost_x_behind, ghost_x_here = ghost_x_here, ghost_x_ahead
    if lags:
        lag_a, lag_b = more[-2:]
        even = gx % 2 == 0
        for n, ref in enumerate((u_ref, u_out)[2 - lags :]):
            for k in range(LAG):
                head = ref[2, k, pl.ds(0, 32)]
                tail = ref[2, k + XS - LAG, pl.ds(0, 32)]
                lag_a[n, k] = jnp.where(even, tail, head)
                lag_b[n, k] = jnp.where(even, head, tail)
    if last:
        for x in range(XS):
            more[0][x] = u_out[2, x]
        return
    strip_out, coupling_out, xa_out, xb_out = more[:4]
    static = [static_ref[pl.ds(SOLID * k, SOLID)] for k in range(3)]
    old = [old_ref[pl.ds(SOLID * c, SOLID)] for c in range(3)]
    strips = strip_step(
        strips, old, static[0], static[1], static[2] == 1.0, bottom, strip_before, strip_after
    )
    for c in range(3):
        strip_out[pl.ds(SOLID * c, SOLID)] = strips[c]
    send_strip_faces(strips, xa_out, xb_out, pl.ds(FACE, SOLID))
    send_faces(lambda c, x: u_out[c, x], lambda x: p_out[x], xa_out, xb_out)
    bottom, velocity = coupling(
        half,
        lambda x: velocity_of(u_out[2, x], u_ref[2, x], d_ref[x]),
        lambda x: p_out[x],
    )
    coupling_out[pl.ds(0, SOLID)] = bottom
    coupling_out[pl.ds(SOLID, SOLID)] = velocity


def own_range(lag):
    return max(0, LAG - lag), min(XS, XS + LAG - lag)


def open_pairs():
    pairs = []
    for lag in range(2 * LAG + 1):
        low, high = own_range(lag)
        pairs.extend((lag, x) for x in range(XS) if not low <= x < high)
    return {pair: at for at, pair in enumerate(pairs)}


def lag_halos(a, b):
    gx = lax.axis_index("gx")
    even = gx % 2 == 0
    before = jnp.where(gx > 0, jnp.where(even, b, a), 0.0)
    after = jnp.where(gx < lax.axis_size("gx") - 1, jnp.where(even, a, b), 0.0)
    return before, after


def image_kernel(
    u0, u1, u2, u3, first_a, first_b, third_a, third_b, recv_ref,
    out_hbm, open_ref, halo, weights, stage, sems,
):
    for t, (a_ref, b_ref, n) in enumerate(
        ((first_a, first_b, 0), (first_a, first_b, 1), (third_a, third_b, 0))
    ):
        for k in range(LAG):
            halo[t, k], halo[t, LAG + k] = lag_halos(a_ref[n, k], b_ref[n, k])
    for t in range(STEPS):
        for x in range(XS):
            weights[t, x] = recv_ref[t, x].astype(F32)

    def column(t, x):
        if x < 0:
            return halo[t, x + LAG]
        if x >= XS:
            return halo[t, x - XS + LAG]
        if t == STEPS - 1:
            return u3[x]
        return (u0, u1, u2)[t][2, x, pl.ds(0, OWN)]

    pairs = open_pairs()
    copies = []
    for lag in range(2 * LAG + 1):
        low, high = own_range(lag)
        for x in range(XS):
            at = x + lag - LAG
            total = column(0, at) * weights[0, x]
            total = total + column(1, at) * weights[1, x]
            total = total + column(2, at) * weights[2, x]
            if low <= x < high:
                total = total + column(3, at) * weights[3, x]
                stage[lag, x] = total.astype(jnp.bfloat16)
            else:
                open_ref[pairs[lag, x]] = total
        columns = pl.ds(low, high - low)
        copy = pltpu.make_async_copy(
            stage.at[lag, columns], out_hbm.at[lag, columns], sems.at[lag]
        )
        copy.start()
        copies.append(copy)
    for copy in copies:
        copy.wait()


def finish_kernel(with_a, open_ref, got_ref, recv_ref, image_hbm, out_hbm, stage, sems):
    gx = lax.axis_index("gx")
    beyond = (gx % 2 == 0) == with_a
    pairs = open_pairs()

    def finish(after):
        present = gx < lax.axis_size("gx") - 1 if after else gx > 0
        copies = []
        for n in range(LAG):
            lag = LAG + 1 + n if after else n
            low, high = own_range(lag)
            start, stop = (high, XS) if after else (0, low)
            for x in range(start, stop):
                plane = got_ref[0, x + lag - LAG - XS if after else x + lag]
                plane = jnp.where(present, plane, 0.0)
                total = open_ref[pairs[lag, x]] + plane * recv_ref[STEPS - 1, x].astype(F32)
                stage[n, x] = total.astype(jnp.bfloat16)
            columns = pl.ds(start, stop - start)
            copy = pltpu.make_async_copy(
                stage.at[n, columns], out_hbm.at[lag, columns], sems.at[n]
            )
            copy.start()
            copies.append(copy)
        for copy in copies:
            copy.wait()

    pl.when(beyond)(lambda: finish(True))
    pl.when(jnp.logical_not(beyond))(lambda: finish(False))


def call(body, outs, *args, specs=None, scratch=(), limit=40):
    return pl.pallas_call(
        body,
        out_shape=[jax.ShapeDtypeStruct(shape, F32) for shape in outs],
        in_specs=specs or [VMEM] * len(args),
        out_specs=[VMEM] * len(outs),
        scratch_shapes=list(scratch),
        compiler_params=pltpu.CompilerParams(vmem_limit_bytes=int(limit * 1024 * 1024)),
    )(*args)


def swapped(size, width):
    return [(i, i ^ width) for i in range(size)]


def crossed(size, width):
    return [(i, (((i + width) % size ^ width) - width) % size) for i in range(size)]


def on_device(p_now, p_prev, water_coef, seafloor, u_now, u_prev, shear, bulk, recv_field):
    size_x = lax.axis_size("gx")
    size_y = lax.axis_size("gy")
    half = lax.axis_index("gy") % 2
    far = jnp.where(half == 0, 4 * DEPTH, -4 * DEPTH)
    levels = jnp.where(seafloor >= 0, seafloor, far)[:, :, None]
    depth = jnp.arange(1, DEPTH + 1, dtype=jnp.int32)[None, None, :]
    field = (depth - levels).astype(F32)
    pressures = jnp.stack([p_now, p_prev, water_coef])
    raw = (field, u_now, u_prev, jnp.stack([shear, bulk]), pressures)
    tile = (XS, 8, DEPTH)
    y_payload = (4,) + tile
    w_payload = (XS + XS // 2, 8, DEPTH)
    hbm = pl.BlockSpec(memory_space=pltpu.HBM)
    *masked, ya, yb, w_out, to_partner = call(
        pack_kernel,
        [u_now.shape, u_now.shape, shear.shape, shear.shape, y_payload, y_payload, w_payload, (INNER + 9 * OWN, DEPTH)],
        *raw,
        specs=[VMEM, hbm, hbm, VMEM, VMEM],
        scratch=[pltpu.SemaphoreType.DMA((2,))],
        limit=PACK_LIMIT,
    )

    def to_y(first, second):
        return (
            lax.ppermute(first, "gy", swapped(size_y, 2)),
            lax.ppermute(second, "gy", crossed(size_y, 2)),
        )

    partner = lax.ppermute(to_partner, "gy", swapped(size_y, 1))
    ya, yb = to_y(ya, yb)
    w_out = lax.ppermute(w_out, "gy", crossed(size_y, 1))
    y_strip = (SOLID, DEPTH)
    full, ysa, ysb = call(strip_kernel, [(9 * OWN, DEPTH), y_strip, y_strip], to_partner, partner)
    ysa, ysb = to_y(ysa, ysb)
    solid = (XS, SOLID, DEPTH)
    water = (XS, WATER, DEPTH)
    face = (FACE + SOLID, DEPTH)
    strip = (3 * SOLID, DEPTH)
    pair = (2 * SOLID, DEPTH)
    u, v, s, b, d, p, q, c, now, old, static, own, xa, xb = call(
        assemble_kernel,
        [(3,) + solid, (3,) + solid, solid, solid, solid, water, water, water,
         strip, strip, strip, pair, face, face],
        field, *masked, pressures, ya, yb, w_out, partner, full, ysa, ysb,
    )

    def to_x(first, second):
        return (
            lax.ppermute(first, "gx", swapped(size_x, 1)),
            lax.ppermute(second, "gx", crossed(size_x, 1)),
        )

    got = lax.ppermute(own, "gy", swapped(size_y, 1))
    faces = to_x(xa, xb)
    verticals, reaches = [], []
    for t in range(STEPS):
        last = t == STEPS - 1
        lags = (0, 2, 1, 1)[t]
        if last:
            outs = [(3, XS, 32, DEPTH), (XS, 16, DEPTH), (XS, 32, DEPTH)]
        else:
            outs = [(3,) + solid, water, strip, pair, face, face]
        outs = outs + [(lags, LAG, 32, DEPTH)] * (2 if lags else 0)

        def body(*refs, last=last, lags=lags):
            step_kernel(last, lags, *refs)

        u_new, p_new, *more = call(
            body, outs, u, v, s, b, d, p, q, c, now, old, static, own, got, *faces
        )
        v, u, q, p = u, u_new, p, p_new
        if last:
            verticals.append(more[0])
        else:
            verticals.append(u)
            old, now, own = now, more[0], more[1]
            faces = to_x(more[2], more[3])
            got = lax.ppermute(own, "gy", swapped(size_y, 1))
        if lags:
            reaches += to_x(more[-2], more[-1])
    lags = 2 * LAG + 1
    image_shape = jax.ShapeDtypeStruct((lags, XS, OWN, DEPTH), jnp.bfloat16)
    open_shape = jax.ShapeDtypeStruct((len(open_pairs()), OWN, DEPTH), F32)
    stage = pltpu.VMEM(image_shape.shape, jnp.bfloat16)
    image, unfinished = pl.pallas_call(
        image_kernel,
        out_shape=[image_shape, open_shape],
        in_specs=[VMEM] * 9,
        out_specs=[hbm, VMEM],
        scratch_shapes=[
            pltpu.VMEM((STEPS - 1, 2 * LAG, OWN, DEPTH), F32),
            pltpu.VMEM((STEPS, XS, OWN, DEPTH), F32),
            stage,
            pltpu.SemaphoreType.DMA((lags,)),
        ],
        compiler_params=PARAMS,
    )(*verticals, *reaches[0:4], recv_field)
    for with_a, got in ((True, reaches[4]), (False, reaches[5])):

        def finish(*refs, with_a=with_a):
            finish_kernel(with_a, *refs)

        image = pl.pallas_call(
            finish,
            out_shape=image_shape,
            in_specs=[VMEM] * 3 + [hbm],
            out_specs=hbm,
            scratch_shapes=[
                pltpu.VMEM((LAG, XS, OWN, DEPTH), jnp.bfloat16),
                pltpu.SemaphoreType.DMA((LAG,)),
            ],
            input_output_aliases={3: 0},
            compiler_params=PARAMS,
        )(unfinished, got, recv_field, image)
    return (p, u, image)


def solution(mesh):
    return jax.shard_map(
        on_device,
        mesh=mesh,
        in_specs=(
            P("gx", "gy", None),
            P("gx", "gy", None),
            P("gx", "gy", None),
            P("gx", "gy"),
            P(None, "gx", "gy", None),
            P(None, "gx", "gy", None),
            P("gx", "gy", None),
            P("gx", "gy", None),
            P(None, "gx", "gy", None),
        ),
        out_specs=(P("gx", "gy", None), P(None, "gx", "gy", None), P(None, "gx", "gy", None)),
        check_vma=False,
    )
```

```python
import jax
import jax.numpy as jnp
from jax import lax
from jax.experimental import pallas as pl
from jax.experimental.pallas import tpu as pltpu
from jax.sharding import PartitionSpec as P

LAG = 10
STEPS = 4
LOAD = 0.5
F32 = jnp.float32
XS = 16
SOLID = 40
WATER = 24
DEPTH = 128
FACE = 3 * SOLID + WATER
OWN = 32
INNER = 192
VMEM = pl.BlockSpec(memory_space=pltpu.VMEM)
PACK_LIMIT = 49.5
PARAMS = pltpu.CompilerParams(vmem_limit_bytes=40 * 1024 * 1024)


def iota(shape, dim):
    return lax.broadcasted_iota(jnp.int32, shape, dim)


def turned(value, shift, axis):
    return pltpu.roll(value, shift % value.shape[axis], axis)


def after_y(value):
    return turned(value, -1, 0)


def before_y(value):
    return turned(value, 1, 0)


def after_z(value, ghost):
    return jnp.where(iota(value.shape, 1) == DEPTH - 1, ghost, turned(value, -1, 1))


def before_z(value, ghost):
    return jnp.where(iota(value.shape, 1) == 0, ghost, turned(value, 1, 1))


def coordinates():
    gx = lax.axis_index("gx")
    gy = lax.axis_index("gy")
    return gx, gy // 2, gy % 2


def coupling(half, vn_of, water_of):
    group = iota((SOLID, DEPTH), 1) // 8
    group_w = iota((WATER, DEPTH), 1) // 8
    sub = iota((8, DEPTH), 0)
    velocity = jnp.zeros((SOLID, DEPTH), F32)
    bottom = jnp.zeros((WATER, DEPTH), F32)
    for x in range(XS):
        velocity = jnp.where(group == x, vn_of(x), velocity)
        bottom = jnp.where(group_w == x, water_of(x)[:, DEPTH - 1 : DEPTH], bottom)
    low = half == 0
    zero = jnp.zeros((8, DEPTH), F32)
    own0, own1, own2 = bottom[0:8], bottom[8:16], bottom[16:24]
    keep = (sub < 4) != low
    spread = jnp.concatenate(
        [
            jnp.where(low, own0, zero),
            jnp.where(low, own1, zero),
            jnp.where(low, zero, own0),
            jnp.where(low, zero, own1),
            jnp.where(keep, own2, zero),
        ],
        axis=0,
    )
    return spread, velocity


def own_strip(half, plane_of):
    lane = iota((OWN, DEPTH), 1)
    group = lane // 8
    strip = jnp.zeros((OWN, DEPTH), F32)
    for x in range(XS):
        strip = jnp.where(group == x, turned(plane_of(x), 8 * x + 4, 1), strip)
    return jnp.where((lane % 8 < 4) == (half == 0), strip, 0.0)


def send_strip_faces(strips, a_ref, b_ref, rows):
    even = lax.axis_index("gx") % 2 == 0
    group = iota((SOLID, DEPTH), 1) // 8
    head = tail = jnp.zeros((SOLID, DEPTH), F32)
    for c in range(3):
        head = jnp.where(group == c, turned(strips[c], 8 * c, 1), head)
        tail = jnp.where(group == c, turned(strips[c], 8 * c + 8, 1), tail)
    a_ref[rows] = jnp.where(even, tail, head)
    b_ref[rows] = jnp.where(even, head, tail)


def strip_step(now, old, s, b, contact, pb, before, after):
    lane = iota((SOLID, DEPTH), 1)

    def next_x(value, face):
        return jnp.where(lane >= DEPTH - 8, turned(face, DEPTH - 8, 1), turned(value, -8, 1))

    def prev_x(value, face):
        return jnp.where(lane < 8, face, turned(value, 8, 1))

    def next_z(value):
        return turned(value, -1, 1)

    def prev_z(value):
        return turned(value, 1, 1)

    def x_weight(u1, u2):
        return (after_y(u1) - before_y(u1)) + (next_z(u2) - prev_z(u2))

    shifts = []
    for c in range(3):
        u = now[c]
        shifts.append((
            (next_x(u, after[c]), prev_x(u, before[c])),
            (after_y(u), before_y(u)),
            (next_z(u), prev_z(u)),
        ))
    q = [shifts[c][c][0] - shifts[c][c][1] for c in range(3)]
    wx, wy, wz = q[1] + q[2], q[0] + q[2], q[0] + q[1]
    mixed = [
        next_x(wx, x_weight(after[1], after[2])) - prev_x(wx, x_weight(before[1], before[2])),
        after_y(wy) - before_y(wy),
        next_z(wz) - prev_z(wz),
    ]
    new = []
    for c in range(3):
        u = now[c]
        two = u + u
        sums = [up + down for up, down in shifts[c]]
        laplace = (sums[0] + sums[1] + sums[2]) - 6.0 * u
        grad = (sums[c] - two) + 0.25 * mixed[c]
        value = (two - old[c]) + s * laplace + b * grad
        if c == 2:
            value = value - jnp.where(contact, LOAD * pb, 0.0)
        new.append(value)
    return new


def velocity_of(now, before, contact_field):
    return jnp.sum(
        jnp.where(contact_field == 1.0, now - before, 0.0), axis=1, keepdims=True
    )


def paired(first, second, swap):
    return jnp.where(swap, first, turned(second, 4, 0))


def pack_kernel(
    d_ref, un_hbm, up_hbm, elastic, pressures,
    un, up, s_v, b_v, ya_ref, yb_ref, wo_ref, partner_ref, sems,
):
    gx, block, half = coordinates()
    even = block % 2 == 0
    upper = half == 0
    copies = []
    for k, (src, dst) in enumerate(
        ((un_hbm, un), (up_hbm, up))
    ):
        copy = pltpu.make_async_copy(src, dst, sems.at[k])
        copy.start()
        copies.append(copy)
    pn, pp, c_v = (pressures.at[k] for k in range(3))
    sub = iota((8, DEPTH), 0)
    low = sub < 4
    for inner in (True, False):
        keep = low == (upper != inner)

        def pick(ref, at):
            return jnp.where(upper == inner, ref[at, pl.ds(8, 8)], ref[at, pl.ds(0, 8)])

        tiles = [paired(pick(pn, x), pick(pp, x), keep) for x in range(XS)]
        tiles += [paired(pick(c_v, x), pick(c_v, x + 8), keep) for x in range(8)]
        for at, tile in enumerate(tiles):
            if inner:
                partner_ref[pl.ds(8 * at, 8)] = tile
            else:
                wo_ref[at] = tile
    for x in range(XS):
        inside = d_ref[x] >= 1.0
        s_v[x] = jnp.where(inside, elastic[0, x], 0.0)
        b_v[x] = jnp.where(inside, elastic[1, x], 0.0)
    for k, plane_of in enumerate((lambda x: s_v[x], lambda x: b_v[x], lambda x: d_ref[x])):
        partner_ref[pl.ds(INNER + OWN * (6 + k), OWN)] = own_strip(half, plane_of)
    for copy in copies:
        copy.wait()
    for x in range(XS):
        inside = d_ref[x] >= 1.0
        for ref in (un, up):
            for c in range(3):
                ref[c, x] = jnp.where(inside, ref[c, x], 0.0)
        sides = []
        for side, rows in ((0, pl.ds(0, 8)), (1, pl.ds(24, 8))):
            d = d_ref[x, rows]
            u = [un[c, x, rows] for c in range(3)]
            v = [up[c, x, rows] for c in range(3)]
            spare = 3 if side == 0 else 4
            for c in range(3):
                row = c if side == 0 else 5 + c
                v[c] = jnp.where(sub == spare, turned(d, spare - row, 0), v[c])
            keep = low if side == 0 else jnp.logical_not(low)
            sides.append(
                [paired(u[0], u[1], keep), paired(u[2], v[0], keep),
                 paired(v[1], v[2], keep), paired(s_v[x, rows], b_v[x, rows], keep)]
            )
        for k in range(4):
            head, tail = sides[0][k], sides[1][k]
            ya_ref[k, x] = jnp.where(even, tail, head)
            yb_ref[k, x] = jnp.where(even, head, tail)
    planes = [lambda x, c=c: un[c, x] for c in range(3)]
    planes += [lambda x, c=c: up[c, x] for c in range(3)]
    for k, plane_of in enumerate(planes):
        partner_ref[pl.ds(INNER + OWN * k, OWN)] = own_strip(half, plane_of)


def strip_kernel(own_ref, got_ref, full_ref, ya_ref, yb_ref):
    gx, block, half = coordinates()
    even = block % 2 == 0
    low = iota((8, DEPTH), 0) < 4
    full_ref[...] = own_ref[pl.ds(INNER, 9 * OWN)] + got_ref[pl.ds(INNER, 9 * OWN)]
    for pair in range(5):
        first, second = 2 * pair, min(2 * pair + 1, 8)
        sides = []
        for row, keep in ((0, low), (OWN - 8, jnp.logical_not(low))):
            sides.append(
                paired(full_ref[pl.ds(OWN * first + row, 8)], full_ref[pl.ds(OWN * second + row, 8)], keep)
            )
        ya_ref[pl.ds(8 * pair, 8)] = jnp.where(even, sides[1], sides[0])
        yb_ref[pl.ds(8 * pair, 8)] = jnp.where(even, sides[0], sides[1])


def send_faces(solid_of, water_of, a_ref, b_ref):
    even = lax.axis_index("gx") % 2 == 0
    for c in range(3):
        head, tail = solid_of(c, 0), solid_of(c, XS - 1)
        a_ref[pl.ds(SOLID * c, SOLID)] = jnp.where(even, tail, head)
        b_ref[pl.ds(SOLID * c, SOLID)] = jnp.where(even, head, tail)
    head, tail = water_of(0), water_of(XS - 1)
    a_ref[pl.ds(3 * SOLID, WATER)] = jnp.where(even, tail, head)
    b_ref[pl.ds(3 * SOLID, WATER)] = jnp.where(even, head, tail)


def received(a_ref, b_ref, rows):
    gx = lax.axis_index("gx")
    even = gx % 2 == 0
    a, b = a_ref[rows], b_ref[rows]
    before = jnp.where(gx > 0, jnp.where(even, b, a), 0.0)
    after = jnp.where(gx < lax.axis_size("gx") - 1, jnp.where(even, a, b), 0.0)
    return before, after


def assemble_kernel(
    d_ref, un_ref, up_ref, s_ref, b_ref, pressures,
    ya_ref, yb_ref, wo_ref, partner_ref, full_ref, ysa_ref, ysb_ref,
    u_out, v_out, s_out, b_out, d_out, p_out, q_out, c_out, now_out, old_out, static_out, coupling_out, xa_out, xb_out,
):
    gx, block, half = coordinates()
    even = block % 2 == 0
    sub = iota((8, DEPTH), 0)
    low = sub < 4
    has_before = block > 0
    has_after = block < lax.axis_size("gy") // 2 - 1
    outer = jnp.where(half == 0, has_before, has_after)
    own, beyond = pl.ds(0, OWN), pl.ds(OWN, 8)

    def halos(got_a, got_b):
        from_before = jnp.where(has_before, jnp.where(even, got_b, got_a), 0.0)
        from_after = jnp.where(has_after, jnp.where(even, got_a, got_b), 0.0)
        return (
            jnp.where(low, from_after, from_before),
            turned(jnp.where(low, from_before, from_after), 4, 0),
        )

    strip_halos = []
    for pair in range(5):
        rows = pl.ds(8 * pair, 8)
        strip_halos.extend(halos(ysa_ref[rows], ysb_ref[rows]))
    for k in range(9):
        ref = (now_out, old_out, static_out)[k // 3]
        ref[pl.ds(SOLID * (k % 3), OWN)] = full_ref[pl.ds(OWN * k, OWN)]
        ref[pl.ds(SOLID * (k % 3) + OWN, 8)] = strip_halos[k]
    for x in range(XS):
        for c in range(3):
            u_out[c, x, own] = un_ref[c, x]
            v_out[c, x, own] = up_ref[c, x]
        s_out[x, own] = s_ref[x]
        b_out[x, own] = b_ref[x]
        d_out[x, own] = d_ref[x]
        halo = []
        for k in range(4):
            halo.extend(halos(ya_ref[k, x], yb_ref[k, x]))
        contact_rows = jnp.zeros((8, DEPTH), F32)
        for c in range(3):
            v = halo[3 + c]
            contact_rows = jnp.where(sub == c, turned(v, c - 3, 0), contact_rows)
            contact_rows = jnp.where(sub == 5 + c, turned(v, 1 + c, 0), contact_rows)
        halo.append(contact_rows)
        for c in range(3):
            u_out[c, x, beyond] = halo[c]
            v_out[c, x, beyond] = halo[3 + c]
        s_out[x, beyond] = halo[6]
        b_out[x, beyond] = halo[7]
        d_out[x, beyond] = halo[8]
        pn_ref, pp_ref, c_ref = (pressures.at[k] for k in range(3))
        from_partner = low == (half == 0)

        def water_halo(at, natural):
            inner, beyond_it = partner_ref[pl.ds(8 * at, 8)], jnp.where(outer, wo_ref[at], 0.0)
            if not natural:
                inner, beyond_it = turned(inner, 4, 0), turned(beyond_it, 4, 0)
            return jnp.where(from_partner, inner, beyond_it)

        for ref, out, at, natural in (
            (pn_ref, p_out, x, True), (pp_ref, q_out, x, False), (c_ref, c_out, XS + x % 8, x < 8)
        ):
            out[x, pl.ds(0, 16)] = ref[x]
            out[x, pl.ds(16, 8)] = water_halo(at, natural)
    bottom, velocity = coupling(
        half,
        lambda x: velocity_of(u_out[2, x], v_out[2, x], d_out[x]),
        lambda x: p_out[x],
    )
    coupling_out[pl.ds(0, SOLID)] = bottom
    coupling_out[pl.ds(SOLID, SOLID)] = velocity
    strips = [now_out[pl.ds(SOLID * c, SOLID)] for c in range(3)]
    send_strip_faces(strips, xa_out, xb_out, pl.ds(FACE, SOLID))
    send_faces(lambda c, x: u_out[c, x], lambda x: p_out[x], xa_out, xb_out)


def step_kernel(last, lags, early, *refs):
    u_ref, v_ref, s_ref, b_ref, d_ref, p_ref, q_ref, c_ref = refs[0:8]
    now_ref, old_ref, static_ref, own_ref, got_ref, xa_ref, xb_ref = refs[8:15]
    strip_rows = pl.ds(FACE, SOLID)
    u_out, p_out = refs[15 + early : 17 + early]
    more = refs[17 + early :]
    gx, block, half = coordinates()
    low_half = half == 0
    shape = (SOLID, DEPTH)
    lane = iota(shape, 1)
    facing = lane % 8 == jnp.where(low_half, 4, 5)
    sub = iota((8, DEPTH), 0)
    bottom = own_ref[pl.ds(0, SOLID)] + got_ref[pl.ds(0, SOLID)]
    velocity = own_ref[pl.ds(SOLID, SOLID)] + got_ref[pl.ds(SOLID, SOLID)]
    strips = [now_ref[pl.ds(SOLID * c, SOLID)] for c in range(3)]
    strip_before, strip_after = [], []
    for value, out in zip(received(xa_ref, xb_ref, strip_rows), (strip_before, strip_after)):
        out.extend(turned(value, -8 * c, 1) if c else value for c in range(3))

    def of_half(value):
        return jnp.where(facing, jnp.where(low_half, value, turned(value, 2, 1)), 0.0)

    ghosts = [[of_half(v) for v in group] for group in (strip_before, strips, strip_after)]

    def ghost(c, x):
        if x < 0:
            source, shift = ghosts[0][c], 123
        elif x >= XS:
            source, shift = ghosts[2][c], 123
        else:
            source, shift = ghosts[1][c], 123 - 8 * x
        return turned(source, shift, 1)

    faces = [received(xa_ref, xb_ref, pl.ds(SOLID * c, SOLID)) for c in range(3)]
    faces.append(received(xa_ref, xb_ref, pl.ds(3 * SOLID, WATER)))

    def solid(c, x):
        if x < 0:
            return faces[c][0]
        if x >= XS:
            return faces[c][1]
        return u_ref[c, x]

    def water(x):
        if x < 0:
            return faces[3][0]
        if x >= XS:
            return faces[3][1]
        return p_ref[x]

    def plane(x):
        uy, uz = solid(1, x), solid(2, x)
        gz = ghost(2, x)
        up, down = after_y(uy), before_y(uy)
        deep, shallow = after_z(uz, gz), before_z(uz, gz)
        return up - down, up + down, deep - shallow, deep + shallow

    behind = plane(-1)
    here = plane(0)
    ghost_x_behind, ghost_x_here = ghost(0, -1), ghost(0, 0)
    for x in range(XS):
        ahead = plane(x + 1)
        ghost_x_ahead = ghost(0, x + 1)
        qy, sy_y, qz, sz_z = here
        now = [solid(c, x) for c in range(3)]
        nxt = [solid(c, x + 1) for c in range(3)]
        prv = [solid(c, x - 1) for c in range(3)]
        qx = nxt[0] - prv[0]
        sum_x = [nxt[c] + prv[c] for c in range(3)]
        dx = (ahead[0] + ahead[2]) - (behind[0] + behind[2])
        wy = qx + qz
        dy = after_y(wy) - before_y(wy)
        gy_here = ghost(1, x)
        wz = qx + qy
        ghost_wz = (ghost_x_ahead - ghost_x_behind) + (after_y(gy_here) - before_y(gy_here))
        dz = after_z(wz, ghost_wz) - before_z(wz, ghost_wz)
        sum_y = [after_y(now[0]) + before_y(now[0]), sy_y, after_y(now[2]) + before_y(now[2])]
        sum_z = [
            after_z(now[0], ghost_x_here) + before_z(now[0], ghost_x_here),
            after_z(now[1], gy_here) + before_z(now[1], gy_here),
            sz_z,
        ]
        own_sums = [sum_x[0], sum_y[1], sum_z[2]]
        mixed = [dx, dy, dz]
        s, b = s_ref[x], b_ref[x]
        d = d_ref[x]
        contact = d == 1.0
        pb = jnp.broadcast_to(bottom[:, 8 * x : 8 * x + 1], shape)
        vn = jnp.broadcast_to(velocity[:, 8 * x : 8 * x + 1], shape)
        for c in range(3):
            u = now[c]
            two = u + u
            laplace = (sum_x[c] + sum_y[c] + sum_z[c]) - 6.0 * u
            grad = (own_sums[c] - two) + 0.25 * mixed[c]
            new = (two - v_ref[c, x]) + s * laplace + b * grad
            if c == 2:
                new = new - jnp.where(contact, LOAD * pb, 0.0)
            if last:
                u_out[c, x] = new[0:32]
            else:
                u_out[c, x] = new
        beyond = jnp.where(
            sub < 4,
            jnp.where(low_half, vn[16:24], vn[32:40]),
            jnp.where(low_half, vn[32:40], vn[8:16]),
        )
        vn_water = jnp.concatenate([jnp.where(low_half, vn[0:16], vn[16:32]), beyond], axis=0)
        p = water(x)
        lateral = water(x + 1) + water(x - 1) + after_y(p) + before_y(p)
        vertical = after_z(p, p - vn_water) + before_z(p, 0.0)
        p_new = (2.0 * p - q_ref[x]) + c_ref[x] * (lateral + vertical - 6.0 * p)
        if last:
            p_out[x] = p_new[0:16]
        else:
            p_out[x] = p_new
        behind, here = here, ahead
        ghost_x_behind, ghost_x_here = ghost_x_here, ghost_x_ahead
    if lags:
        lag_a, lag_b = more[-2:]
        even = gx % 2 == 0
        for n, ref in enumerate((u_ref, u_out)[2 - lags :]):
            for k in range(LAG):
                head = ref[2, k, pl.ds(0, 32)]
                tail = ref[2, k + XS - LAG, pl.ds(0, 32)]
                lag_a[n, k] = jnp.where(even, tail, head)
                lag_b[n, k] = jnp.where(even, head, tail)
    if last:
        for x in range(XS):
            more[0][x] = u_out[2, x]
        return
    strip_out, coupling_out, xa_out, xb_out = more[:4]
    static = [static_ref[pl.ds(SOLID * k, SOLID)] for k in range(3)]
    old = [old_ref[pl.ds(SOLID * c, SOLID)] for c in range(3)]
    strips = strip_step(
        strips, old, static[0], static[1], static[2] == 1.0, bottom, strip_before, strip_after
    )
    for c in range(3):
        strip_out[pl.ds(SOLID * c, SOLID)] = strips[c]
    send_strip_faces(strips, xa_out, xb_out, pl.ds(FACE, SOLID))
    send_faces(lambda c, x: u_out[c, x], lambda x: p_out[x], xa_out, xb_out)
    bottom, velocity = coupling(
        half,
        lambda x: velocity_of(u_out[2, x], u_ref[2, x], d_ref[x]),
        lambda x: p_out[x],
    )
    coupling_out[pl.ds(0, SOLID)] = bottom
    coupling_out[pl.ds(SOLID, SOLID)] = velocity


def own_range(lag):
    return max(0, LAG - lag), min(XS, XS + LAG - lag)


def open_pairs():
    pairs = []
    for lag in range(2 * LAG + 1):
        low, high = own_range(lag)
        pairs.extend((lag, x) for x in range(XS) if not low <= x < high)
    return {pair: at for at, pair in enumerate(pairs)}


def lag_halos(a, b):
    gx = lax.axis_index("gx")
    even = gx % 2 == 0
    before = jnp.where(gx > 0, jnp.where(even, b, a), 0.0)
    after = jnp.where(gx < lax.axis_size("gx") - 1, jnp.where(even, a, b), 0.0)
    return before, after


def image_kernel(
    u0, u1, u2, u3, first_a, first_b, third_a, third_b, recv_ref,
    out_hbm, open_ref, halo, weights, stage, sems,
):
    for t, (a_ref, b_ref, n) in enumerate(
        ((first_a, first_b, 0), (first_a, first_b, 1), (third_a, third_b, 0))
    ):
        for k in range(LAG):
            halo[t, k], halo[t, LAG + k] = lag_halos(a_ref[n, k], b_ref[n, k])
    for t in range(STEPS):
        for x in range(XS):
            weights[t, x] = recv_ref[t, x].astype(F32)

    def column(t, x):
        if x < 0:
            return halo[t, x + LAG]
        if x >= XS:
            return halo[t, x - XS + LAG]
        if t == STEPS - 1:
            return u3[x]
        return (u0, u1, u2)[t][2, x, pl.ds(0, OWN)]

    pairs = open_pairs()
    copies = []
    for lag in range(2 * LAG + 1):
        low, high = own_range(lag)
        for x in range(XS):
            at = x + lag - LAG
            total = column(0, at) * weights[0, x]
            total = total + column(1, at) * weights[1, x]
            total = total + column(2, at) * weights[2, x]
            if low <= x < high:
                total = total + column(3, at) * weights[3, x]
                stage[lag, x] = total.astype(jnp.bfloat16)
            else:
                open_ref[pairs[lag, x]] = total
        columns = pl.ds(low, high - low)
        copy = pltpu.make_async_copy(
            stage.at[lag, columns], out_hbm.at[lag, columns], sems.at[lag]
        )
        copy.start()
        copies.append(copy)
    for copy in copies:
        copy.wait()


def finish_kernel(with_a, open_ref, got_ref, recv_ref, image_hbm, out_hbm, stage, sems):
    gx = lax.axis_index("gx")
    beyond = (gx % 2 == 0) == with_a
    pairs = open_pairs()

    def finish(after):
        present = gx < lax.axis_size("gx") - 1 if after else gx > 0
        copies = []
        for n in range(LAG):
            lag = LAG + 1 + n if after else n
            low, high = own_range(lag)
            start, stop = (high, XS) if after else (0, low)
            for x in range(start, stop):
                plane = got_ref[0, x + lag - LAG - XS if after else x + lag]
                plane = jnp.where(present, plane, 0.0)
                total = open_ref[pairs[lag, x]] + plane * recv_ref[STEPS - 1, x].astype(F32)
                stage[n, x] = total.astype(jnp.bfloat16)
            columns = pl.ds(start, stop - start)
            copy = pltpu.make_async_copy(
                stage.at[n, columns], out_hbm.at[lag, columns], sems.at[n]
            )
            copy.start()
            copies.append(copy)
        for copy in copies:
            copy.wait()

    pl.when(beyond)(lambda: finish(True))
    pl.when(jnp.logical_not(beyond))(lambda: finish(False))


def call(body, outs, *args, specs=None, scratch=(), limit=40):
    return pl.pallas_call(
        body,
        out_shape=[jax.ShapeDtypeStruct(shape, F32) for shape in outs],
        in_specs=specs or [VMEM] * len(args),
        out_specs=[VMEM] * len(outs),
        scratch_shapes=list(scratch),
        compiler_params=pltpu.CompilerParams(vmem_limit_bytes=int(limit * 1024 * 1024)),
    )(*args)


def swapped(size, width):
    return [(i, i ^ width) for i in range(size)]


def crossed(size, width):
    return [(i, (((i + width) % size ^ width) - width) % size) for i in range(size)]


def on_device(p_now, p_prev, water_coef, seafloor, u_now, u_prev, shear, bulk, recv_field):
    size_x = lax.axis_size("gx")
    size_y = lax.axis_size("gy")
    half = lax.axis_index("gy") % 2
    far = jnp.where(half == 0, 4 * DEPTH, -4 * DEPTH)
    levels = jnp.where(seafloor >= 0, seafloor, far)[:, :, None]
    depth = jnp.arange(1, DEPTH + 1, dtype=jnp.int32)[None, None, :]
    field = (depth - levels).astype(F32)
    pressures = jnp.stack([p_now, p_prev, water_coef])
    raw = (field, u_now, u_prev, jnp.stack([shear, bulk]), pressures)
    tile = (XS, 8, DEPTH)
    y_payload = (4,) + tile
    w_payload = (XS + XS // 2, 8, DEPTH)
    hbm = pl.BlockSpec(memory_space=pltpu.HBM)
    *masked, ya, yb, w_out, to_partner = call(
        pack_kernel,
        [u_now.shape, u_now.shape, shear.shape, shear.shape, y_payload, y_payload, w_payload, (INNER + 9 * OWN, DEPTH)],
        *raw,
        specs=[VMEM, hbm, hbm, VMEM, VMEM],
        scratch=[pltpu.SemaphoreType.DMA((2,))],
        limit=PACK_LIMIT,
    )

    def to_y(first, second):
        return (
            lax.ppermute(first, "gy", swapped(size_y, 2)),
            lax.ppermute(second, "gy", crossed(size_y, 2)),
        )

    partner = lax.ppermute(to_partner, "gy", swapped(size_y, 1))
    ya, yb = to_y(ya, yb)
    w_out = lax.ppermute(w_out, "gy", crossed(size_y, 1))
    y_strip = (SOLID, DEPTH)
    full, ysa, ysb = call(strip_kernel, [(9 * OWN, DEPTH), y_strip, y_strip], to_partner, partner)
    ysa, ysb = to_y(ysa, ysb)
    solid = (XS, SOLID, DEPTH)
    water = (XS, WATER, DEPTH)
    face = (FACE + SOLID, DEPTH)
    strip = (3 * SOLID, DEPTH)
    pair = (2 * SOLID, DEPTH)
    u, v, s, b, d, p, q, c, now, old, static, own, xa, xb = call(
        assemble_kernel,
        [(3,) + solid, (3,) + solid, solid, solid, solid, water, water, water,
         strip, strip, strip, pair, face, face],
        field, *masked, pressures, ya, yb, w_out, partner, full, ysa, ysb,
    )

    def to_x(first, second):
        return (
            lax.ppermute(first, "gx", swapped(size_x, 1)),
            lax.ppermute(second, "gx", crossed(size_x, 1)),
        )

    got = lax.ppermute(own, "gy", swapped(size_y, 1))
    faces = to_x(xa, xb)
    verticals, reaches = [], []
    for t in range(STEPS):
        last = t == STEPS - 1
        lags = (0, 2, 1, 1)[t]
        if last:
            outs = [(3, XS, 32, DEPTH), (XS, 16, DEPTH), (XS, 32, DEPTH)]
        else:
            outs = [(3,) + solid, water, strip, pair, face, face]
        outs = outs + [(lags, LAG, 32, DEPTH)] * (2 if lags else 0)

        arrived = reaches[0:1] if t == 2 else []

        def body(*refs, last=last, lags=lags, early=len(arrived)):
            step_kernel(last, lags, early, *refs)

        u_new, p_new, *more = call(
            body, outs, u, v, s, b, d, p, q, c, now, old, static, own, got, *faces, *arrived
        )
        v, u, q, p = u, u_new, p, p_new
        if last:
            verticals.append(more[0])
        else:
            verticals.append(u)
            old, now, own = now, more[0], more[1]
            faces = to_x(more[2], more[3])
            got = lax.ppermute(own, "gy", swapped(size_y, 1))
        if lags:
            reaches += to_x(more[-2], more[-1])
    lags = 2 * LAG + 1
    image_shape = jax.ShapeDtypeStruct((lags, XS, OWN, DEPTH), jnp.bfloat16)
    open_shape = jax.ShapeDtypeStruct((len(open_pairs()), OWN, DEPTH), F32)
    stage = pltpu.VMEM(image_shape.shape, jnp.bfloat16)
    image, unfinished = pl.pallas_call(
        image_kernel,
        out_shape=[image_shape, open_shape],
        in_specs=[VMEM] * 9,
        out_specs=[hbm, VMEM],
        scratch_shapes=[
            pltpu.VMEM((STEPS - 1, 2 * LAG, OWN, DEPTH), F32),
            pltpu.VMEM((STEPS, XS, OWN, DEPTH), F32),
            stage,
            pltpu.SemaphoreType.DMA((lags,)),
        ],
        compiler_params=PARAMS,
    )(*verticals, *reaches[0:4], recv_field)
    for with_a, got in ((True, reaches[4]), (False, reaches[5])):

        def finish(*refs, with_a=with_a):
            finish_kernel(with_a, *refs)

        image = pl.pallas_call(
            finish,
            out_shape=image_shape,
            in_specs=[VMEM] * 3 + [hbm],
            out_specs=hbm,
            scratch_shapes=[
                pltpu.VMEM((LAG, XS, OWN, DEPTH), jnp.bfloat16),
                pltpu.SemaphoreType.DMA((LAG,)),
            ],
            input_output_aliases={3: 0},
            compiler_params=PARAMS,
        )(unfinished, got, recv_field, image)
    return (p, u, image)


def solution(mesh):
    return jax.shard_map(
        on_device,
        mesh=mesh,
        in_specs=(
            P("gx", "gy", None),
            P("gx", "gy", None),
            P("gx", "gy", None),
            P("gx", "gy"),
            P(None, "gx", "gy", None),
            P(None, "gx", "gy", None),
            P("gx", "gy", None),
            P("gx", "gy", None),
            P(None, "gx", "gy", None),
        ),
        out_specs=(P("gx", "gy", None), P(None, "gx", "gy", None), P(None, "gx", "gy", None)),
        check_vma=False,
    )
```
